256 devices in a mesh: ping: 4 (over z_lo), band: 64 (over y, z_hi, x, core).
Axes of the slice: x: 4, y: 4, z: 8 (z_hi: 2, z_lo: 4; z = z_hi * 4 + z_lo), core: 2. Of those that a mesh axis runs over, the one named last changes fastest.
Arguments:
- staves: bfloat16 [2, 64, 256, 8, 512], P(None, 'ping', 'band'), may hold values from -6 to 6
- weights: bfloat16 [2, 256, 512, 512], P(None, 'band'), may hold values from -0.25 to 0.25
- replica: float32 [2, 2048], replicated, may hold values from -5 to 5
- start: int32 [64, 512], P('ping', 'band'), may hold values from 0 to 1535
- length: int32 [64, 512], P('ping', 'band'), may hold values from 64 to 512
Outputs:
- centroid: float32 [64, 512], P('ping', 'band')
- energy: float32 [64, 512], P('ping', 'band')
The draws below stay inside these ranges and needn't reach their ends.
Inputs may be any that keep to these rules, and one draw needn't show every extreme that they name: Every window lies inside the beam's samples: start + length <= 2048.
All inputs are finite; a program needn't handle non-finite values.
Results may differ from the reference program's by a relative error of at most 0.0004.
Values may be sent and summed in bfloat16 or wider, within the bound.
A program may use at most 128 MiB of HBM per device.

```python
import math
import jax
import jax.numpy as jnp
from jax import lax

STAVES = 512
BEAMS = 512
BANDS = 256
BINS = 8
LENGTH = 2048
PINGS = 64


def touch_ends(drawn, rng, least, high):
    longest = drawn.shape.index(max(drawn.shape))
    spots = []
    for shift in (0, 1):
        where = [jax.random.randint(jax.random.fold_in(rng, axis), (), 0, length) for axis, length in enumerate(drawn.shape)]
        where[longest] = (where[longest] + shift) % drawn.shape[longest]
        spots.append(tuple(where))
    return drawn.at[spots[0]].set(least).at[spots[1]].set(high)


def block_levels(rng, shape, shards, least, largest):
    loudness, own = 1.0, jax.random.fold_in(rng, 6)
    for dim, parts in shards:
        heights = jnp.exp(jax.random.uniform(jax.random.fold_in(own, dim), (parts,), jnp.float32, least / len(shards), largest / len(shards)))
        loudness = loudness * jnp.repeat(heights, shape[dim] // parts).reshape([-1 if axis == dim else 1 for axis in range(len(shape))])
    return loudness


def gaussian(key, shape, spread, reach, split=(), kind=jnp.bfloat16):
    values = spread * jax.random.normal(key, shape, jnp.float32)
    if split:
        values = values * block_levels(key, shape, split, -0.22, 0.18)
    return jnp.clip(values, -reach, reach).astype(kind)


def setup_inputs(seed: int = 0) -> dict:
    seeds = jax.random.split(jax.random.key(seed), 6)
    staves = gaussian(seeds[0], (2, PINGS, BANDS, BINS, STAVES), 1.0, 6.0, ((1, 4), (2, 64)))
    weights = gaussian(seeds[1], (2, BANDS, STAVES, BEAMS), STAVES ** -0.5, 0.25, ((1, 64),))
    replica = gaussian(seeds[2], (2, LENGTH), 1.0, 5.0, (), jnp.float32)
    start = touch_ends(jax.random.randint(seeds[3], (PINGS, BEAMS), 0, LENGTH - LENGTH // 4), jax.random.fold_in(seeds[3], 1), 0, (LENGTH - LENGTH // 4) - 1).astype(jnp.int32)
    length = touch_ends(jax.random.randint(seeds[4], (PINGS, BEAMS), LENGTH // 32, LENGTH // 4 + 1), jax.random.fold_in(seeds[4], 1), LENGTH // 32, (LENGTH // 4 + 1) - 1).astype(jnp.int32)
    return {"staves": staves, "weights": weights, "replica": replica, "start": start, "length": length}


TAPS = (1.0, 2.0, 3.0, 4.0, 5.0, 4.0, 3.0, 2.0, 1.0)


def dft_tables(length_total):
    freqs = jnp.arange(length_total, dtype=jnp.int32)
    phases = (freqs[:, None] * freqs[None, :]) % length_total
    angles = phases.astype(jnp.float32) * (2.0 * math.pi / length_total)
    return jnp.cos(angles).astype(jnp.bfloat16), jnp.sin(angles).astype(jnp.bfloat16)


def envelope_rows(spec_re, spec_im, replica, cos_table, sin_table):
    comp_re = (spec_re * replica[0] + spec_im * replica[1]).astype(jnp.bfloat16)
    comp_im = (spec_im * replica[0] - spec_re * replica[1]).astype(jnp.bfloat16)
    wave_re = jnp.dot(comp_re, cos_table, preferred_element_type=jnp.float32) - jnp.dot(comp_im, sin_table, preferred_element_type=jnp.float32)
    wave_im = jnp.dot(comp_re, sin_table, preferred_element_type=jnp.float32) + jnp.dot(comp_im, cos_table, preferred_element_type=jnp.float32)
    return (wave_re * wave_re + wave_im * wave_im) * (1.0 / (16.0 * cos_table.shape[0]))


def beamform_band(operands):
    stave_band, weight_band = operands
    flat_re = stave_band[0].reshape(-1, stave_band.shape[-1])
    flat_im = stave_band[1].reshape(-1, stave_band.shape[-1])
    beam_re = jnp.dot(flat_re, weight_band[0], preferred_element_type=jnp.float32) - jnp.dot(flat_im, weight_band[1], preferred_element_type=jnp.float32)
    beam_im = jnp.dot(flat_re, weight_band[1], preferred_element_type=jnp.float32) + jnp.dot(flat_im, weight_band[0], preferred_element_type=jnp.float32)
    stacked = jnp.stack([beam_re, beam_im]).astype(jnp.bfloat16)
    return stacked.reshape(2, stave_band.shape[1], stave_band.shape[2], weight_band.shape[-1])


def smooth_pings(padded, first_ping, total_pings, ping_count):
    positions = first_ping + jnp.arange(ping_count + 8, dtype=jnp.int32) - 4
    inside = ((positions >= 0) & (positions < total_pings)).astype(jnp.float32)
    summed = jnp.zeros(padded.shape[:0] + (ping_count,) + padded.shape[1:], jnp.float32)
    weight_sum = jnp.zeros((ping_count,), jnp.float32)
    for offset in range(9):
        summed = summed + TAPS[offset] * padded[offset:offset + ping_count]
        weight_sum = weight_sum + TAPS[offset] * inside[offset:offset + ping_count]
    return summed / weight_sum[:, None, None]


def window_stats(smoothed, start, length):
    samples = jnp.arange(smoothed.shape[-1], dtype=jnp.int32)
    window_start = start[..., None]
    finish = (start + length)[..., None]
    inside = (samples >= window_start) & (samples < finish)
    offsets = samples.astype(jnp.float32) - start.astype(jnp.float32)[..., None] + 0.5
    energy_total = jnp.sum(jnp.where(inside, smoothed, 0.0), axis=-1)
    moment = jnp.sum(jnp.where(inside, smoothed * offsets, 0.0), axis=-1)
    widths = length.astype(jnp.float32)
    return moment / (widths * (energy_total + 1e-6)), energy_total / widths


def reference(staves, weights, replica, start, length):
    beams = lax.map(beamform_band, (jnp.moveaxis(staves, 2, 0), jnp.moveaxis(weights, 1, 0)))
    spectra = jnp.transpose(beams, (1, 2, 4, 0, 3)).reshape(2, PINGS, BEAMS, LENGTH)
    cos_table, sin_table = dft_tables(LENGTH)

    def per_ping(spectrum):
        return envelope_rows(spectrum[0].astype(jnp.float32), spectrum[1].astype(jnp.float32), replica, cos_table, sin_table)

    envelope = lax.map(per_ping, jnp.moveaxis(spectra, 1, 0))
    padded = jnp.pad(envelope, ((4, 4), (0, 0), (0, 0)))
    smoothed = smooth_pings(padded, 0, PINGS, PINGS)
    centroid, energy = window_stats(smoothed, start, length)
    return (centroid, energy)
```

```python
import functools
import math

import ml_dtypes
import numpy as np

import jax
import jax.numpy as jnp
from jax import lax
from jax.experimental import pallas as pl
from jax.experimental.pallas import tpu as pltpu
from jax.sharding import PartitionSpec as P

MESH = pl.DeviceIdType.MESH
BINS, SPLIT, REACH = 8, 256, 4
TAPS = (1.0, 2.0, 3.0, 4.0, 5.0, 4.0, 3.0, 2.0, 1.0)


def tables(sources, bands_each):
    total = SPLIT * BINS
    turn = 2.0 * math.pi / total
    t1 = np.arange(SPLIT)
    band = (np.arange(sources)[None, :] * bands_each + np.arange(bands_each)[:, None]).reshape(-1)
    angle = ((t1[:, None] * band[None, :] * BINS) % total) * turn
    first = np.block([[np.cos(angle), -np.sin(angle)], [np.sin(angle), np.cos(angle)]])
    lane = np.arange(128)
    ping, small = lane // BINS, lane % BINS
    angle = ((t1[:, None] * small[None, :]) % total) * turn
    twiddle = np.stack([np.cos(angle), np.sin(angle)])
    same = ping[:, None] == ping[None, :]
    angle = ((small[:, None] * small[None, :]) % BINS) * (2.0 * math.pi / BINS)
    cos, sin = np.cos(angle) * same, np.sin(angle) * same
    second = np.block([[cos, sin], [-sin, cos]])
    above, below = ping + 16, ping - 16
    beside = np.where(ping < REACH, above, np.where(ping >= 16 - REACH, below, 1000))
    target = np.concatenate([ping, beside])
    kind = np.concatenate([small, small])
    smooth = np.maximum(5 - np.abs(ping[:, None] - target[None, :]), 0) * (small[:, None] == kind[None, :])
    half = ml_dtypes.bfloat16
    return first.astype(half), twiddle.astype(np.float32), second.astype(half), smooth.astype(half)


def kernel(
    bands, blocks,
    staves, weights, rep, win, length, first_in, twiddle_in, second_in, smooth_in,
    centroid, energy,
    xbuf, wbuf, sbuf, rbuf, fbuf, rhs, first, twiddle, second, smooth, near, acc, hrecv,
    xsem, wsem, csem, ssem, rsem, nsem, msem, hsem, gsem,
):
    me, block = lax.axis_index("band"), lax.axis_index("ping")
    each = wbuf.shape[0]

    loads = []
    for k in range(each):
        loads.append([
            pltpu.make_async_copy(staves.at[:, :, k], xbuf.at[k], xsem.at[k]),
            pltpu.make_async_copy(weights.at[:, k], wbuf.at[k], wsem.at[k]),
        ])
        for copy in loads[-1]:
            copy.start()
    consts = [
        pltpu.make_async_copy(a, b, csem.at[i])
        for i, (a, b) in enumerate([(first_in, first), (twiddle_in, twiddle), (second_in, second), (smooth_in, smooth)])
    ]
    for copy in consts:
        copy.start()

    near[...] = jnp.zeros_like(near)
    hrecv[...] = jnp.zeros_like(hrecv)

    barrier = pltpu.get_barrier_semaphore()

    @pl.loop(1, bands)
    def _(i):
        pl.semaphore_signal(barrier, inc=1, device_id={"band": lax.rem(me + i, bands)}, device_id_type=MESH)

    @pl.when(block > 0)
    def _():
        pl.semaphore_signal(barrier, inc=1, device_id={"ping": block - 1}, device_id_type=MESH)

    @pl.when(block < blocks - 1)
    def _():
        pl.semaphore_signal(barrier, inc=1, device_id={"ping": block + 1}, device_id_type=MESH)

    sides = (block > 0).astype(jnp.int32) + (block < blocks - 1).astype(jnp.int32)

    def beside(src, dst, up_sems, down_sems):
        up = pltpu.make_async_remote_copy(
            src, dst.at[0], up_sems.at[0], down_sems.at[0], device_id={"ping": block + 1}, device_id_type=MESH)
        down = pltpu.make_async_remote_copy(
            src, dst.at[1], up_sems.at[1], down_sems.at[1], device_id={"ping": block - 1}, device_id_type=MESH)
        return up, down

    def send(copies):
        @pl.when(block < blocks - 1)
        def _():
            copies[0].start()

        @pl.when(block > 0)
        def _():
            copies[1].start()

    def receive(copies):
        @pl.when(block > 0)
        def _():
            copies[0].wait_recv()

        @pl.when(block < blocks - 1)
        def _():
            copies[1].wait_recv()

    def sent(copies):
        @pl.when(block < blocks - 1)
        def _():
            copies[0].wait_send()

        @pl.when(block > 0)
        def _():
            copies[1].wait_send()

    edges = beside(win, near, nsem, msem)

    for k in range(each):
        for copy in loads[k]:
            copy.wait()
        x = xbuf[k].astype(jnp.float32).reshape(2 * 128, -1).astype(jnp.bfloat16)
        r0, r1 = rep[k, 0:1, :], rep[k, 1:2, :]
        columns = wbuf.shape[-1]
        width = 256
        for c in range(columns // width):
            here = pl.ds(c * width, width)
            p0 = jnp.dot(x, wbuf[k, 0, :, here], preferred_element_type=jnp.float32)
            p1 = jnp.dot(x, wbuf[k, 1, :, here], preferred_element_type=jnp.float32)
            re = (p0[:128] - p1[128:]).astype(jnp.bfloat16).T.astype(jnp.float32)
            im = (p1[:128] + p0[128:]).astype(jnp.bfloat16).T.astype(jnp.float32)
            cre = (re * r0 + im * r1).reshape(width // 8, 8, 128)
            cim = (im * r0 - re * r1).reshape(width // 8, 8, 128)
            sbuf[k, pl.ds(c * (width // 8), width // 8)] = jnp.concatenate([cre, cim], axis=1).astype(jnp.bfloat16)
        if k == 0:
            pl.semaphore_wait(barrier, bands - 1 + sides)
            send(edges)

        @pl.loop(1, bands)
        def _(i):
            other = lax.rem(me + i, bands)
            pltpu.make_async_remote_copy(
                sbuf.at[k, other], rbuf.at[k, me], ssem.at[k], rsem.at[k],
                device_id={"band": other}, device_id_type=MESH,
            ).start()

        rbuf[k, me] = sbuf[k, me]

    for k in range(each):
        pltpu.make_async_remote_copy(
            sbuf.at[k, pl.ds(0, bands - 1)], rbuf.at[k, pl.ds(0, bands - 1)], ssem.at[k], rsem.at[k],
            device_id={"band": lax.rem(me + 1, bands)}, device_id_type=MESH,
        ).wait_recv()
        fbuf[k] = rbuf[k].astype(jnp.float32).reshape(bands * 16, 128)

    for copy in consts:
        copy.wait()
    receive(edges)

    lane = lax.broadcasted_iota(jnp.int32, (16, 128), 1)
    wide = jnp.where(lane < 8 * REACH, near[1], jnp.where(lane >= 128 - 8 * REACH, near[0], 4096.0))
    near[0] = wide
    rows = lax.broadcasted_iota(jnp.int32, (SPLIT, 1), 0).astype(jnp.float32)

    @pl.loop(0, 4)
    def _(pair):
        for i in range(2):
            for j in range(each):
                for h in range(2):
                    part = fbuf[j, pl.ds(i * 8 + pair * 2 + h, bands, stride=16), :]
                    rhs[pl.ds((i * each + j) * bands, bands), h * 128 : (h + 1) * 128] = part.astype(jnp.bfloat16)
        y = jnp.dot(first[...], rhs[...], preferred_element_type=jnp.float32)
        for h in range(2):
            b = pair * 2 + h
            yr, yi = y[:SPLIT, h * 128 : (h + 1) * 128], y[SPLIT:, h * 128 : (h + 1) * 128]
            c, s = twiddle[0], twiddle[1]
            z = jnp.concatenate([yr * c - yi * s, yr * s + yi * c], axis=1).astype(jnp.bfloat16)
            w = jnp.dot(z, second[...], preferred_element_type=jnp.float32)
            wr, wi = w[:, :128], w[:, 128:]
            env = (wr * wr + wi * wi).astype(jnp.bfloat16)
            smoothed = jnp.dot(env, smooth[...], preferred_element_type=jnp.float32)
            for g in range(2):
                sm = smoothed[:, g * 128 : (g + 1) * 128]
                source = win if g == 0 else near.at[0]
                low, high = source[pl.ds(b, 1), :], source[pl.ds(b + 8, 1), :]
                v = jnp.where((rows >= low) & (rows < high), sm, 0.0)
                e = jnp.sum(v, axis=0, keepdims=True)
                m = jnp.sum(v * rows, axis=0, keepdims=True) + (0.5 - low) * e
                acc[g, pl.ds(b, 1), :] = e
                acc[g, pl.ds(b + 8, 1), :] = m

    partial = beside(acc.at[1], hrecv, hsem, gsem)
    send(partial)
    receive(partial)
    total = acc[0] + jnp.where(lane < 8 * REACH, hrecv[0], 0.0) + jnp.where(lane >= 128 - 8 * REACH, hrecv[1], 0.0)
    rowp = lax.broadcasted_iota(jnp.int32, (16, 128), 0)
    group = jnp.where(lane // 8 == rowp, 1.0, 0.0)
    both = lax.dot_general(
        group, total, (((1,), (1,)), ((), ())), precision=lax.Precision.HIGHEST, preferred_element_type=jnp.float32)
    place = block * 16 + lax.broadcasted_iota(jnp.int32, (16, 8), 0)
    weight = jnp.zeros((16, 8), jnp.float32)
    for j, tap in enumerate(TAPS):
        q = place + (j - REACH)
        weight = weight + jnp.where((q >= 0) & (q < blocks * 16), tap, 0.0)
    scale = (1.0 / (16.0 * SPLIT * BINS)) / weight
    e, m = both[:, :8] * scale, both[:, 8:] * scale
    widths = length[...]
    centroid[...] = m / (widths * (e + 1e-06))
    energy[...] = e / widths

    sent(edges)
    sent(partial)
    for k in range(each):
        pltpu.make_async_remote_copy(
            sbuf.at[k, pl.ds(0, bands - 1)], rbuf.at[k, pl.ds(0, bands - 1)], ssem.at[k], rsem.at[k],
            device_id={"band": lax.rem(me + 1, bands)}, device_id_type=MESH,
        ).wait_send()


def local(bands, blocks, staves, weights, replica, start, length):
    me = lax.axis_index("band")
    each = weights.shape[1]
    first, twiddle, second, smooth = tables(bands, each)
    own = lax.dynamic_slice_in_dim(replica, me * (each * BINS), each * BINS, axis=1)
    rep = jnp.broadcast_to(own.reshape(2, each, 1, BINS), (2, each, 16, BINS)).reshape(2, each, 128).swapaxes(0, 1)
    low = start.T.astype(jnp.float32)[:, :, None] - 256.0 * jnp.arange(8, dtype=jnp.float32)
    high = low + length.T.astype(jnp.float32)[:, :, None]
    win = jnp.concatenate([low.reshape(8, 128), high.reshape(8, 128)], axis=0)
    vmem, hbm = pl.BlockSpec(memory_space=pltpu.VMEM), pl.BlockSpec(memory_space=pl.ANY)
    f32, bf16, dma = jnp.float32, jnp.bfloat16, pltpu.SemaphoreType.DMA
    out = jax.ShapeDtypeStruct((16, 8), f32)
    return pl.pallas_call(
        functools.partial(kernel, bands, blocks),
        out_shape=(out, out),
        in_specs=[hbm, hbm, vmem, vmem, vmem, hbm, hbm, hbm, hbm],
        out_specs=(vmem, vmem),
        scratch_shapes=[
            pltpu.VMEM((each, 2, 16, 8, 512), bf16),
            pltpu.VMEM((each, 2, 512, 512), bf16),
            pltpu.VMEM((each, bands, 16, 128), bf16),
            pltpu.VMEM((each, bands, 16, 128), bf16),
            pltpu.VMEM((each, bands * 16, 128), f32),
            pltpu.VMEM((2 * each * bands, 256), bf16),
            pltpu.VMEM(first.shape, bf16),
            pltpu.VMEM(twiddle.shape, f32),
            pltpu.VMEM(second.shape, bf16),
            pltpu.VMEM(smooth.shape, bf16),
            pltpu.VMEM((2, 16, 128), f32),
            pltpu.VMEM((2, 16, 128), f32),
            pltpu.VMEM((2, 16, 128), f32),
            dma((each,)), dma((each,)), dma((4,)), dma((each,)), dma((each,)),
            dma((2,)), dma((2,)), dma((2,)), dma((2,)),
        ],
        compiler_params=pltpu.CompilerParams(collective_id=0, has_side_effects=True, vmem_limit_bytes=48 << 20),
    )(staves, weights, rep, win, length.astype(f32), first, twiddle, second, smooth)


def solution(mesh):
    in_specs = (
        P(None, "ping", "band", None, None),
        P(None, "band", None, None),
        P(),
        P("ping", "band"),
        P("ping", "band"),
    )
    out_specs = (P("ping", "band"), P("ping", "band"))
    step = functools.partial(local, mesh.shape["band"], mesh.shape["ping"])
    return jax.shard_map(step, mesh=mesh, in_specs=in_specs, out_specs=out_specs, check_vma=False)
```

```python
import functools
import math

import ml_dtypes
import numpy as np

import jax
import jax.numpy as jnp
from jax import lax
from jax.experimental import pallas as pl
from jax.experimental.pallas import tpu as pltpu
from jax.sharding import PartitionSpec as P

MESH = pl.DeviceIdType.MESH
BINS, SPLIT, REACH = 8, 256, 4
TAPS = (1.0, 2.0, 3.0, 4.0, 5.0, 4.0, 3.0, 2.0, 1.0)


def tables(sources, bands_each):
    total = SPLIT * BINS
    turn = 2.0 * math.pi / total
    t1 = np.arange(SPLIT)
    band = (np.arange(sources)[None, :] * bands_each + np.arange(bands_each)[:, None]).reshape(-1)
    angle = ((t1[:, None] * band[None, :] * BINS) % total) * turn
    first = np.block([[np.cos(angle), -np.sin(angle)], [np.sin(angle), np.cos(angle)]])
    lane = np.arange(128)
    ping, small = lane // BINS, lane % BINS
    angle = ((t1[:, None] * small[None, :]) % total) * turn
    twiddle = np.stack([np.cos(angle), np.sin(angle)])
    same = ping[:, None] == ping[None, :]
    angle = ((small[:, None] * small[None, :]) % BINS) * (2.0 * math.pi / BINS)
    cos, sin = np.cos(angle) * same, np.sin(angle) * same
    second = np.block([[cos, sin], [-sin, cos]])
    above, below = ping + 16, ping - 16
    beside = np.where(ping < REACH, above, np.where(ping >= 16 - REACH, below, 1000))
    target = np.concatenate([ping, beside])
    kind = np.concatenate([small, small])
    smooth = np.maximum(5 - np.abs(ping[:, None] - target[None, :]), 0) * (small[:, None] == kind[None, :])
    half = ml_dtypes.bfloat16
    return first.astype(half), twiddle.astype(np.float32), second.astype(half), smooth.astype(half)


def kernel(
    bands, blocks,
    staves, weights, replica, start, length, first_in, twiddle_in, second_in, smooth_in,
    centroid, energy,
    qbuf, tbuf, rep, win, xbuf, wbuf, sbuf, rbuf, fbuf, rhs, first, twiddle, second, smooth, near, acc, hrecv,
    qsem, xsem, wsem, csem, ssem, rsem, nsem, msem, hsem, gsem,
):
    me, block = lax.axis_index("band"), lax.axis_index("ping")
    each = wbuf.shape[0]

    small = [
        pltpu.make_async_copy(a, b, qsem.at[i])
        for i, (a, b) in enumerate([(replica, qbuf), (start, tbuf.at[0]), (length, tbuf.at[1])])
    ]
    for copy in small:
        copy.start()
    loads = []
    for k in range(each):
        loads.append([
            pltpu.make_async_copy(staves.at[:, :, k], xbuf.at[k], xsem.at[k]),
            pltpu.make_async_copy(weights.at[:, k], wbuf.at[k], wsem.at[k]),
        ])
        for copy in loads[-1]:
            copy.start()
    consts = [
        pltpu.make_async_copy(a, b, csem.at[i])
        for i, (a, b) in enumerate([(first_in, first), (twiddle_in, twiddle), (second_in, second), (smooth_in, smooth)])
    ]
    for copy in consts:
        copy.start()

    near[...] = jnp.zeros_like(near)
    hrecv[...] = jnp.zeros_like(hrecv)

    barrier = pltpu.get_barrier_semaphore()

    @pl.loop(1, bands)
    def _(i):
        pl.semaphore_signal(barrier, inc=1, device_id={"band": lax.rem(me + i, bands)}, device_id_type=MESH)

    @pl.when(block > 0)
    def _():
        pl.semaphore_signal(barrier, inc=1, device_id={"ping": block - 1}, device_id_type=MESH)

    @pl.when(block < blocks - 1)
    def _():
        pl.semaphore_signal(barrier, inc=1, device_id={"ping": block + 1}, device_id_type=MESH)

    sides = (block > 0).astype(jnp.int32) + (block < blocks - 1).astype(jnp.int32)

    def beside(src, dst, up_sems, down_sems):
        up = pltpu.make_async_remote_copy(
            src, dst.at[0], up_sems.at[0], down_sems.at[0], device_id={"ping": block + 1}, device_id_type=MESH)
        down = pltpu.make_async_remote_copy(
            src, dst.at[1], up_sems.at[1], down_sems.at[1], device_id={"ping": block - 1}, device_id_type=MESH)
        return up, down

    def send(copies):
        @pl.when(block < blocks - 1)
        def _():
            copies[0].start()

        @pl.when(block > 0)
        def _():
            copies[1].start()

    def receive(copies):
        @pl.when(block > 0)
        def _():
            copies[0].wait_recv()

        @pl.when(block < blocks - 1)
        def _():
            copies[1].wait_recv()

    def sent(copies):
        @pl.when(block < blocks - 1)
        def _():
            copies[0].wait_send()

        @pl.when(block > 0)
        def _():
            copies[1].wait_send()

    edges = beside(win, near, nsem, msem)

    for copy in small:
        copy.wait()
    span = each * BINS
    spread = functools.partial(jnp.dot, precision=lax.Precision.HIGHEST, preferred_element_type=jnp.float32)
    row, column = (lax.broadcasted_iota(jnp.int32, (128, 128), d) for d in (0, 1))
    per_tile = 128 // span
    part = qbuf[:, pl.ds(pl.multiple_of(lax.div(me, per_tile) * 128, 128), 128)]
    for k in range(each):
        pick = jnp.where(row == lax.rem(me, per_tile) * span + k * BINS + lax.rem(column, BINS), 1.0, 0.0)
        rep[k] = spread(part, pick)
    row, column = (lax.broadcasted_iota(jnp.int32, (16, 128), d) for d in (0, 1))
    pick = jnp.where(row == lax.div(column, BINS), 1.0, 0.0)
    times = spread(tbuf[...].astype(jnp.float32).reshape(16, 16), pick)
    low = times[:8] - (lax.rem(column[:8], BINS) * SPLIT).astype(jnp.float32)
    win[0:8] = low
    win[8:16] = low + times[8:]

    for k in range(each):
        for copy in loads[k]:
            copy.wait()
        x = xbuf[k].astype(jnp.float32).reshape(2 * 128, -1).astype(jnp.bfloat16)
        r0, r1 = rep[k, 0:1, :], rep[k, 1:2, :]
        columns = wbuf.shape[-1]
        width = 256
        for c in range(columns // width):
            here = pl.ds(c * width, width)
            p0 = jnp.dot(x, wbuf[k, 0, :, here], preferred_element_type=jnp.float32)
            p1 = jnp.dot(x, wbuf[k, 1, :, here], preferred_element_type=jnp.float32)
            re = (p0[:128] - p1[128:]).astype(jnp.bfloat16).T.astype(jnp.float32)
            im = (p1[:128] + p0[128:]).astype(jnp.bfloat16).T.astype(jnp.float32)
            cre = (re * r0 + im * r1).reshape(width // 8, 8, 128)
            cim = (im * r0 - re * r1).reshape(width // 8, 8, 128)
            sbuf[k, pl.ds(c * (width // 8), width // 8)] = jnp.concatenate([cre, cim], axis=1).astype(jnp.bfloat16)
        if k == 0:
            pl.semaphore_wait(barrier, bands - 1 + sides)
            send(edges)

        @pl.loop(1, bands)
        def _(i):
            other = lax.rem(me + i, bands)
            pltpu.make_async_remote_copy(
                sbuf.at[k, other], rbuf.at[k, me], ssem.at[k], rsem.at[k],
                device_id={"band": other}, device_id_type=MESH,
            ).start()

        rbuf[k, me] = sbuf[k, me]

    for k in range(each):
        pltpu.make_async_remote_copy(
            sbuf.at[k, pl.ds(0, bands - 1)], rbuf.at[k, pl.ds(0, bands - 1)], ssem.at[k], rsem.at[k],
            device_id={"band": lax.rem(me + 1, bands)}, device_id_type=MESH,
        ).wait_recv()
        fbuf[k] = rbuf[k].astype(jnp.float32).reshape(bands * 16, 128)

    for copy in consts:
        copy.wait()
    receive(edges)

    lane = lax.broadcasted_iota(jnp.int32, (16, 128), 1)
    wide = jnp.where(lane < 8 * REACH, near[1], jnp.where(lane >= 128 - 8 * REACH, near[0], 4096.0))
    near[0] = wide
    rows = lax.broadcasted_iota(jnp.int32, (SPLIT, 1), 0).astype(jnp.float32)

    @pl.loop(0, 4)
    def _(pair):
        for i in range(2):
            for j in range(each):
                for h in range(2):
                    part = fbuf[j, pl.ds(i * 8 + pair * 2 + h, bands, stride=16), :]
                    rhs[pl.ds((i * each + j) * bands, bands), h * 128 : (h + 1) * 128] = part.astype(jnp.bfloat16)
        y = jnp.dot(first[...], rhs[...], preferred_element_type=jnp.float32)
        for h in range(2):
            b = pair * 2 + h
            yr, yi = y[:SPLIT, h * 128 : (h + 1) * 128], y[SPLIT:, h * 128 : (h + 1) * 128]
            c, s = twiddle[0], twiddle[1]
            z = jnp.concatenate([yr * c - yi * s, yr * s + yi * c], axis=1).astype(jnp.bfloat16)
            w = jnp.dot(z, second[...], preferred_element_type=jnp.float32)
            wr, wi = w[:, :128], w[:, 128:]
            env = (wr * wr + wi * wi).astype(jnp.bfloat16)
            smoothed = jnp.dot(env, smooth[...], preferred_element_type=jnp.float32)
            for g in range(2):
                sm = smoothed[:, g * 128 : (g + 1) * 128]
                source = win if g == 0 else near.at[0]
                low, high = source[pl.ds(b, 1), :], source[pl.ds(b + 8, 1), :]
                v = jnp.where((rows >= low) & (rows < high), sm, 0.0)
                e = jnp.sum(v, axis=0, keepdims=True)
                m = jnp.sum(v * rows, axis=0, keepdims=True) + (0.5 - low) * e
                acc[g, pl.ds(b, 1), :] = e
                acc[g, pl.ds(b + 8, 1), :] = m

    partial = beside(acc.at[1], hrecv, hsem, gsem)
    send(partial)
    receive(partial)
    total = acc[0] + jnp.where(lane < 8 * REACH, hrecv[0], 0.0) + jnp.where(lane >= 128 - 8 * REACH, hrecv[1], 0.0)
    rowp = lax.broadcasted_iota(jnp.int32, (16, 128), 0)
    group = jnp.where(lane // 8 == rowp, 1.0, 0.0)
    both = lax.dot_general(
        total, group, (((1,), (1,)), ((), ())), precision=lax.Precision.HIGHEST, preferred_element_type=jnp.float32)
    place = block * 16 + lax.broadcasted_iota(jnp.int32, (8, 16), 1)
    weight = jnp.zeros((8, 16), jnp.float32)
    for j, tap in enumerate(TAPS):
        q = place + (j - REACH)
        weight = weight + jnp.where((q >= 0) & (q < blocks * 16), tap, 0.0)
    scale = (1.0 / (16.0 * SPLIT * BINS)) / weight
    e, m = both[:8] * scale, both[8:] * scale
    widths = tbuf[1].astype(jnp.float32)
    centroid[...] = m / (widths * (e + 1e-06))
    energy[...] = e / widths

    sent(edges)
    sent(partial)
    for k in range(each):
        pltpu.make_async_remote_copy(
            sbuf.at[k, pl.ds(0, bands - 1)], rbuf.at[k, pl.ds(0, bands - 1)], ssem.at[k], rsem.at[k],
            device_id={"band": lax.rem(me + 1, bands)}, device_id_type=MESH,
        ).wait_send()


def local(bands, blocks, staves, weights, replica, start, length):
    each = weights.shape[1]
    first, twiddle, second, smooth = tables(bands, each)
    vmem, hbm = pl.BlockSpec(memory_space=pltpu.VMEM), pl.BlockSpec(memory_space=pltpu.HBM)
    f32, bf16, dma = jnp.float32, jnp.bfloat16, pltpu.SemaphoreType.DMA
    out = jax.ShapeDtypeStruct((8, 16), f32)
    centroid, energy = pl.pallas_call(
        functools.partial(kernel, bands, blocks),
        out_shape=(out, out),
        in_specs=[hbm] * 9,
        out_specs=(vmem, vmem),
        scratch_shapes=[
            pltpu.VMEM(replica.shape, f32),
            pltpu.VMEM((2, 8, 16), jnp.int32),
            pltpu.VMEM((each, 2, 128), f32),
            pltpu.VMEM((16, 128), f32),
            pltpu.VMEM((each, 2, 16, 8, 512), bf16),
            pltpu.VMEM((each, 2, 512, 512), bf16),
            pltpu.VMEM((each, bands, 16, 128), bf16),
            pltpu.VMEM((each, bands, 16, 128), bf16),
            pltpu.VMEM((each, bands * 16, 128), f32),
            pltpu.VMEM((2 * each * bands, 256), bf16),
            pltpu.VMEM(first.shape, bf16),
            pltpu.VMEM(twiddle.shape, f32),
            pltpu.VMEM(second.shape, bf16),
            pltpu.VMEM(smooth.shape, bf16),
            pltpu.VMEM((2, 16, 128), f32),
            pltpu.VMEM((2, 16, 128), f32),
            pltpu.VMEM((2, 16, 128), f32),
            dma((3,)), dma((each,)), dma((each,)), dma((4,)), dma((each,)), dma((each,)),
            dma((2,)), dma((2,)), dma((2,)), dma((2,)),
        ],
        compiler_params=pltpu.CompilerParams(collective_id=0, has_side_effects=True, vmem_limit_bytes=63 << 20),
    )(staves, weights, replica, start.T, length.T, first, twiddle, second, smooth)
    return centroid.T, energy.T


def solution(mesh):
    in_specs = (
        P(None, "ping", "band", None, None),
        P(None, "band", None, None),
        P(),
        P("ping", "band"),
        P("ping", "band"),
    )
    out_specs = (P("ping", "band"), P("ping", "band"))
    step = functools.partial(local, mesh.shape["band"], mesh.shape["ping"])
    return jax.shard_map(step, mesh=mesh, in_specs=in_specs, out_specs=out_specs, check_vma=False)
```

```python
import functools
import math

import ml_dtypes
import numpy as np

import jax
import jax.numpy as jnp
from jax import lax
from jax.experimental import pallas as pl
from jax.experimental.pallas import tpu as pltpu
from jax.sharding import PartitionSpec as P

MESH = pl.DeviceIdType.MESH
BINS, SPLIT, REACH = 8, 256, 4
ROW = 8
TAPS = (1.0, 2.0, 3.0, 4.0, 5.0, 4.0, 3.0, 2.0, 1.0)


def tables(sources, bands_each):
    total = SPLIT * BINS
    turn = 2.0 * math.pi / total
    t1 = np.arange(SPLIT)
    half_of, plane = np.divmod(np.arange(sources), sources // 2)
    source = (plane // ROW * 2 + half_of) * ROW + plane % ROW
    band = (source[None, :] * bands_each + np.arange(bands_each)[:, None]).reshape(-1)
    angle = ((t1[:, None] * band[None, :] * BINS) % total) * turn
    first = np.block([[np.cos(angle), -np.sin(angle)], [np.sin(angle), np.cos(angle)]])
    lane = np.arange(128)
    ping, small = lane // BINS, lane % BINS
    angle = ((t1[:, None] * small[None, :]) % total) * turn
    twiddle = np.stack([np.cos(angle), np.sin(angle)])
    same = ping[:, None] == ping[None, :]
    angle = ((small[:, None] * small[None, :]) % BINS) * (2.0 * math.pi / BINS)
    cos, sin = np.cos(angle) * same, np.sin(angle) * same
    second = np.block([[cos, sin], [-sin, cos]])
    above, below = ping + 16, ping - 16
    beside = np.where(ping < REACH, above, np.where(ping >= 16 - REACH, below, 1000))
    target = np.concatenate([ping, beside])
    kind = np.concatenate([small, small])
    smooth = np.maximum(5 - np.abs(ping[:, None] - target[None, :]), 0) * (small[:, None] == kind[None, :])
    half = ml_dtypes.bfloat16
    return first.astype(half), twiddle.astype(np.float32), second.astype(half), smooth.astype(half)


def kernel(
    bands, blocks,
    staves, weights, replica, start, length, first_in, twiddle_in, second_in, smooth_in,
    result,
    qbuf, tbuf, rep, win, xbuf, wbuf, sbuf, over, gathered, plane, beyond, fbuf, rhs, ebuf,
    first, twiddle, second, smooth, near, acc, hrecv,
    qsem, xsem, wsem, csem, psend, precv, zsend, zrecv, nsem, msem, hsem, gsem,
):
    me, block = lax.axis_index("band"), lax.axis_index("ping")
    each = wbuf.shape[0]
    columns = bands // (2 * ROW)
    here_z = lax.rem(lax.div(me, ROW), 2)
    there_z = 1 - here_z
    y, r = lax.div(me, 2 * ROW), lax.rem(me, ROW)
    mine = y * ROW + r

    def at(y, z, r):
        return {"band": (y * 2 + z) * ROW + r}

    near[...] = jnp.zeros_like(near)
    hrecv[...] = jnp.zeros_like(hrecv)

    barrier = pltpu.get_barrier_semaphore()
    pl.semaphore_signal(barrier, inc=1, device_id=at(y, there_z, r), device_id_type=MESH)

    @pl.loop(1, columns * ROW)
    def _(i):
        place = lax.rem(mine + i, columns * ROW)
        pl.semaphore_signal(
            barrier, inc=1, device_id=at(lax.div(place, ROW), here_z, lax.rem(place, ROW)), device_id_type=MESH)

    @pl.when(block > 0)
    def _():
        pl.semaphore_signal(barrier, inc=1, device_id={"ping": block - 1}, device_id_type=MESH)

    @pl.when(block < blocks - 1)
    def _():
        pl.semaphore_signal(barrier, inc=1, device_id={"ping": block + 1}, device_id_type=MESH)

    loads = []
    for k in range(each):
        loads.append([
            pltpu.make_async_copy(staves.at[:, :, k], xbuf.at[k], xsem.at[k]),
            pltpu.make_async_copy(weights.at[:, k], wbuf.at[k], wsem.at[k]),
        ])
        for copy in loads[-1]:
            copy.start()
        if k == 0:
            small = [
                pltpu.make_async_copy(a, b, qsem.at[i])
                for i, (a, b) in enumerate([(replica, qbuf), (start, tbuf.at[0]), (length, tbuf.at[1])])
            ]
            for copy in small:
                copy.start()
    consts = [
        pltpu.make_async_copy(a, b, csem.at[i])
        for i, (a, b) in enumerate([(first_in, first), (twiddle_in, twiddle), (second_in, second), (smooth_in, smooth)])
    ]
    for copy in consts:
        copy.start()

    def across(src, dst, n):
        return pltpu.make_async_remote_copy(
            src, dst, zsend.at[n], zrecv.at[n], device_id=at(y, there_z, r), device_id_type=MESH)

    size = columns * ROW

    def scatter(src, dst, n):
        @pl.loop(1, size)
        def _(i):
            place = lax.rem(mine + i, size)
            pltpu.make_async_remote_copy(
                src.at[place], dst.at[mine], psend.at[n], precv.at[n],
                device_id=at(lax.div(place, ROW), here_z, lax.rem(place, ROW)), device_id_type=MESH,
            ).start()

        dst[mine] = src[mine]

    def scattered(src, dst, n):
        rest = pl.ds(0, size - 1)
        return pltpu.make_async_remote_copy(
            src.at[rest], dst.at[rest], psend.at[n], precv.at[n],
            device_id=at(y, here_z, lax.rem(r + 1, ROW)), device_id_type=MESH)

    sides = (block > 0).astype(jnp.int32) + (block < blocks - 1).astype(jnp.int32)

    def beside(src, dst, up_sems, down_sems):
        up = pltpu.make_async_remote_copy(
            src, dst.at[0], up_sems.at[0], down_sems.at[0], device_id={"ping": block + 1}, device_id_type=MESH)
        down = pltpu.make_async_remote_copy(
            src, dst.at[1], up_sems.at[1], down_sems.at[1], device_id={"ping": block - 1}, device_id_type=MESH)
        return up, down

    def send(copies):
        @pl.when(block < blocks - 1)
        def _():
            copies[0].start()

        @pl.when(block > 0)
        def _():
            copies[1].start()

    def receive(copies):
        @pl.when(block > 0)
        def _():
            copies[0].wait_recv()

        @pl.when(block < blocks - 1)
        def _():
            copies[1].wait_recv()

    def sent(copies):
        @pl.when(block < blocks - 1)
        def _():
            copies[0].wait_send()

        @pl.when(block > 0)
        def _():
            copies[1].wait_send()

    edges = beside(win, near, nsem, msem)

    for copy in small:
        copy.wait()
    span = each * BINS
    spread = functools.partial(jnp.dot, precision=lax.Precision.HIGHEST, preferred_element_type=jnp.float32)
    row, column = (lax.broadcasted_iota(jnp.int32, (128, 128), d) for d in (0, 1))
    per_tile = 128 // span
    part = qbuf[:, pl.ds(pl.multiple_of(lax.div(me, per_tile) * 128, 128), 128)]
    for k in range(each):
        pick = jnp.where(row == lax.rem(me, per_tile) * span + k * BINS + lax.rem(column, BINS), 1.0, 0.0)
        rep[k] = spread(part, pick)
    row, column = (lax.broadcasted_iota(jnp.int32, (16, 128), d) for d in (0, 1))
    pick = jnp.where(row == lax.div(column, BINS), 1.0, 0.0)
    times = spread(tbuf[...].astype(jnp.float32).reshape(16, 16), pick)
    low = times[:8] - (lax.rem(column[:8], BINS) * SPLIT).astype(jnp.float32)
    win[0:8] = low
    win[8:16] = low + times[8:]

    def beams(k, c):
        x = xbuf[k].astype(jnp.float32).reshape(2 * 128, -1).astype(jnp.bfloat16)
        r0, r1 = rep[k, 0:1, :], rep[k, 1:2, :]
        here = pl.ds(c * 256, 256)
        p0 = jnp.dot(x, wbuf[k, 0, :, here], preferred_element_type=jnp.float32)
        p1 = jnp.dot(x, wbuf[k, 1, :, here], preferred_element_type=jnp.float32)
        re = (p0[:128] - p1[128:]).astype(jnp.bfloat16).T.astype(jnp.float32)
        im = (p1[:128] + p0[128:]).astype(jnp.bfloat16).T.astype(jnp.float32)
        return (re * r0 + im * r1).reshape(32, 8, 128), (im * r0 - re * r1).reshape(32, 8, 128)

    def put(n, c, parts):
        tiles = jnp.concatenate(parts, axis=1).astype(jnp.bfloat16)
        for i in range(4):
            sbuf[n, i % 2, (c * 2 + i // 2) * ROW : (c * 2 + i // 2 + 1) * ROW] = tiles[i * ROW : (i + 1) * ROW]

    chunks = wbuf.shape[-1] // 256

    def early(k):
        for copy in loads[k]:
            copy.wait()
        for c in range(chunks):
            put(k, c, beams(k, c))

    early(0)
    pl.semaphore_wait(barrier, size + sides)
    across(sbuf.at[0, there_z], over.at[0], 0).start()
    send(edges)
    for k in (2, 3):
        for copy in loads[k]:
            copy.wait()
    for c in range(chunks):
        a, b = beams(2, c), beams(3, c)
        for h in range(2):
            part = slice(4 * h, 4 * h + 4)
            put(2 + h, c, [a[0][:, part], b[0][:, part], a[1][:, part], b[1][:, part]])
    for h in range(2):
        scatter(sbuf.at[2 + h, there_z], gathered.at[h], 4 + h)
    early(1)
    across(sbuf.at[1, there_z], over.at[1], 1).start()

    scattered(sbuf.at[2, there_z], gathered.at[0], 4).wait_recv()
    across(gathered.at[0], beyond.at[2], 2).start()
    for n in range(3):
        scatter(sbuf.at[n, here_z], plane.at[n], n)
    across(sbuf.at[0, there_z], over.at[0], 0).wait_recv()
    scatter(over.at[0], beyond.at[0], 6)
    scatter(sbuf.at[3, here_z], plane.at[3], 3)
    scattered(sbuf.at[3, there_z], gathered.at[1], 5).wait_recv()
    across(sbuf.at[1, there_z], over.at[1], 1).wait_recv()
    across(gathered.at[1], beyond.at[3], 3).start()
    scatter(over.at[1], beyond.at[1], 7)

    half = columns * ROW * 16

    def unpack(n, z, tiles):
        fbuf[n, pl.ds(z * half, half)] = tiles.astype(jnp.float32).reshape(half, 128)

    for copy in consts:
        copy.wait()
    receive(edges)
    lane = lax.broadcasted_iota(jnp.int32, (16, 128), 1)
    wide = jnp.where(lane < 8 * REACH, near[1], jnp.where(lane >= 128 - 8 * REACH, near[0], 4096.0))
    near[0] = wide
    rows = lax.broadcasted_iota(jnp.int32, (SPLIT, 1), 0).astype(jnp.float32)

    for k in range(2):
        scattered(sbuf.at[k, here_z], plane.at[k], k).wait_recv()
        unpack(k, here_z, plane[k])
        scattered(over.at[k], beyond.at[k], 6 + k).wait_recv()
        unpack(k, there_z, beyond[k])

    def window(b, g):
        sm = jnp.dot(ebuf[b], smooth[:, g * 128 : (g + 1) * 128], preferred_element_type=jnp.float32)
        source = win if g == 0 else near.at[0]
        low, high = source[pl.ds(b, 1), :], source[pl.ds(b + 8, 1), :]
        v = jnp.where((rows >= low) & (rows < high), sm, 0.0)
        e = jnp.sum(v, axis=0, keepdims=True)
        m = jnp.sum(v * rows, axis=0, keepdims=True) + (0.5 - low) * e
        acc[g, pl.ds(b, 1), :] = e
        acc[g, pl.ds(b + 8, 1), :] = m

    def transform(half_of, pair):
        for i in range(2):
            for j in range(4):
                for h in range(2):
                    q = pair * 2 + h
                    n, at_row = (j, half_of * 4 + q) if j < 2 else (2 + half_of, (j - 2) * 4 + q)
                    part = fbuf[n, pl.ds(i * 8 + at_row, bands, stride=16), :]
                    rhs[pl.ds((i * each + j) * bands, bands), h * 128 : (h + 1) * 128] = part.astype(jnp.bfloat16)
        out = jnp.dot(first[...], rhs[...], preferred_element_type=jnp.float32)
        for h in range(2):
            re, im = out[:SPLIT, h * 128 : (h + 1) * 128], out[SPLIT:, h * 128 : (h + 1) * 128]
            c, s = twiddle[0], twiddle[1]
            z = jnp.concatenate([re * c - im * s, re * s + im * c], axis=1).astype(jnp.bfloat16)
            w = jnp.dot(z, second[...], preferred_element_type=jnp.float32)
            wr, wi = w[:, :128], w[:, 128:]
            ebuf[half_of * 4 + pair * 2 + h] = (wr * wr + wi * wi).astype(jnp.bfloat16)
            window(half_of * 4 + pair * 2 + h, 1)

    partial = beside(acc.at[1], hrecv, hsem, gsem)
    for h in range(2):
        scattered(sbuf.at[2 + h, here_z], plane.at[2 + h], 2 + h).wait_recv()
        unpack(2 + h, here_z, plane[2 + h])
        across(gathered.at[h], beyond.at[2 + h], 2 + h).wait_recv()
        unpack(2 + h, there_z, beyond[2 + h])

        @pl.loop(0, 2)
        def _(pair):
            transform(h, pair)

        if h == 1:
            send(partial)

        @pl.loop(0, 4)
        def _(q):
            window(h * 4 + q, 0)

    receive(partial)
    total = acc[0] + jnp.where(lane < 8 * REACH, hrecv[0], 0.0) + jnp.where(lane >= 128 - 8 * REACH, hrecv[1], 0.0)
    rowp = lax.broadcasted_iota(jnp.int32, (16, 128), 0)
    group = jnp.where(lane // 8 == rowp, 1.0, 0.0)
    both = lax.dot_general(
        total, group, (((1,), (1,)), ((), ())), precision=lax.Precision.HIGHEST, preferred_element_type=jnp.float32)
    place = block * 16 + lax.broadcasted_iota(jnp.int32, (8, 16), 1)
    weight = jnp.zeros((8, 16), jnp.float32)
    for j, tap in enumerate(TAPS):
        q = place + (j - REACH)
        weight = weight + jnp.where((q >= 0) & (q < blocks * 16), tap, 0.0)
    scale = (1.0 / (16.0 * SPLIT * BINS)) / weight
    e, m = both[:8] * scale, both[8:] * scale
    widths = tbuf[1].astype(jnp.float32)
    result[0] = m / (widths * (e + 1e-06))
    result[1] = e / widths

    sent(edges)
    sent(partial)
    for k in range(2):
        scattered(sbuf.at[k, here_z], plane.at[k], k).wait_send()
        scattered(sbuf.at[2 + k, here_z], plane.at[2 + k], 2 + k).wait_send()
        scattered(sbuf.at[2 + k, there_z], gathered.at[k], 4 + k).wait_send()
        scattered(over.at[k], beyond.at[k], 6 + k).wait_send()
        across(sbuf.at[k, there_z], over.at[k], k).wait_send()
        across(gathered.at[k], beyond.at[2 + k], 2 + k).wait_send()


def local(bands, blocks, staves, weights, replica, start, length):
    each = weights.shape[1]
    first, twiddle, second, smooth = tables(bands, each)
    vmem, hbm = pl.BlockSpec(memory_space=pltpu.VMEM), pl.BlockSpec(memory_space=pltpu.HBM)
    f32, bf16, dma = jnp.float32, jnp.bfloat16, pltpu.SemaphoreType.DMA
    plane = (bands // 2, 16, 128)
    out = pl.pallas_call(
        functools.partial(kernel, bands, blocks),
        out_shape=jax.ShapeDtypeStruct((2, 8, 16), f32),
        in_specs=[hbm] * 9,
        out_specs=vmem,
        scratch_shapes=[
            pltpu.VMEM(replica.shape, f32),
            pltpu.VMEM((2, 8, 16), jnp.int32),
            pltpu.VMEM((each, 2, 128), f32),
            pltpu.VMEM((16, 128), f32),
            pltpu.VMEM((each, 2, 16, 8, 512), bf16),
            pltpu.VMEM((each, 2, 512, 512), bf16),
            pltpu.VMEM((each, 2, *plane), bf16),
            pltpu.VMEM((2, *plane), bf16),
            pltpu.VMEM((2, *plane), bf16),
            pltpu.VMEM((each, *plane), bf16),
            pltpu.VMEM((each, *plane), bf16),
            pltpu.VMEM((each, bands * 16, 128), f32),
            pltpu.VMEM((2 * each * bands, 256), bf16),
            pltpu.VMEM((8, SPLIT, 128), bf16),
            pltpu.VMEM(first.shape, bf16),
            pltpu.VMEM(twiddle.shape, f32),
            pltpu.VMEM(second.shape, bf16),
            pltpu.VMEM(smooth.shape, bf16),
            pltpu.VMEM((2, 16, 128), f32),
            pltpu.VMEM((2, 16, 128), f32),
            pltpu.VMEM((2, 16, 128), f32),
            dma((3,)), dma((each,)), dma((each,)), dma((4,)),
            dma((8,)), dma((8,)), dma((each,)), dma((each,)),
            dma((2,)), dma((2,)), dma((2,)), dma((2,)),
        ],
        compiler_params=pltpu.CompilerParams(collective_id=0, has_side_effects=True, vmem_limit_bytes=63 << 20),
    )(staves, weights, replica, start.T, length.T, first, twiddle, second, smooth)
    return out[0].T, out[1].T


def solution(mesh):
    in_specs = (
        P(None, "ping", "band", None, None),
        P(None, "band", None, None),
        P(),
        P("ping", "band"),
        P("ping", "band"),
    )
    out_specs = (P("ping", "band"), P("ping", "band"))
    step = functools.partial(local, mesh.shape["band"], mesh.shape["ping"])
    return jax.shard_map(step, mesh=mesh, in_specs=in_specs, out_specs=out_specs, check_vma=False)
```

```python
import functools
import math

import ml_dtypes
import numpy as np

import jax
import jax.numpy as jnp
from jax import lax
from jax.experimental import pallas as pl
from jax.experimental.pallas import tpu as pltpu
from jax.sharding import PartitionSpec as P

MESH = pl.DeviceIdType.MESH
BINS, SPLIT, REACH = 8, 256, 4
ROW = 8
TAPS = (1.0, 2.0, 3.0, 4.0, 5.0, 4.0, 3.0, 2.0, 1.0)


def tables(sources, bands_each):
    total = SPLIT * BINS
    turn = 2.0 * math.pi / total
    t1 = np.arange(SPLIT)
    place = np.arange(sources // 2)
    first = []
    for z in range(2):
        source = (place // ROW * 2 + z) * ROW + place % ROW
        columns = []
        for pair in range(bands_each // 2):
            band = (source[None, :] * bands_each + pair * 2 + np.arange(2)[:, None]).reshape(-1)
            angle = ((t1[:, None] * band[None, :] * BINS) % total) * turn
            cos, sin = np.cos(angle), np.sin(angle)
            columns.append(np.block([[cos, -sin], [sin, cos]]))
        first.append(np.concatenate(columns, axis=1))
    first = np.stack(first)
    lane = np.arange(128)
    ping, small = lane // BINS, lane % BINS
    angle = ((t1[:, None] * small[None, :]) % total) * turn
    twiddle = np.stack([np.cos(angle), np.sin(angle)])
    same = ping[:, None] == ping[None, :]
    angle = ((small[:, None] * small[None, :]) % BINS) * (2.0 * math.pi / BINS)
    cos, sin = np.cos(angle) * same, np.sin(angle) * same
    second = np.block([[cos, sin], [-sin, cos]])
    above, below = ping + 16, ping - 16
    beside = np.where(ping < REACH, above, np.where(ping >= 16 - REACH, below, 1000))
    target = np.concatenate([ping, beside])
    kind = np.concatenate([small, small])
    smooth = np.maximum(5 - np.abs(ping[:, None] - target[None, :]), 0) * (small[:, None] == kind[None, :])
    half = ml_dtypes.bfloat16
    return first.astype(half), twiddle.astype(np.float32), second.astype(half), smooth.astype(half)


def kernel(
    bands, blocks,
    staves, weights, replica, start, length, first_in, twiddle_in, second_in, smooth_in,
    result,
    qbuf, tbuf, rep, win, xbuf, wbuf, sbuf, over, gathered, plane, beyond, fbuf, rhs, sums, ebuf,
    first, twiddle, second, smooth, near, acc, hrecv,
    qsem, xsem, wsem, csem, psend, precv, zsend, zrecv, nsem, msem, hsem, gsem,
):
    me, block = lax.axis_index("band"), lax.axis_index("ping")
    each = wbuf.shape[0]
    columns = bands // (2 * ROW)
    here_z = lax.rem(lax.div(me, ROW), 2)
    there_z = 1 - here_z
    y, r = lax.div(me, 2 * ROW), lax.rem(me, ROW)
    mine = y * ROW + r

    def at(y, z, r):
        return {"band": (y * 2 + z) * ROW + r}

    near[...] = jnp.zeros_like(near)
    hrecv[...] = jnp.zeros_like(hrecv)

    barrier = pltpu.get_barrier_semaphore()
    pl.semaphore_signal(barrier, inc=1, device_id=at(y, there_z, r), device_id_type=MESH)

    @pl.loop(1, columns * ROW)
    def _(i):
        place = lax.rem(mine + i, columns * ROW)
        pl.semaphore_signal(
            barrier, inc=1, device_id=at(lax.div(place, ROW), here_z, lax.rem(place, ROW)), device_id_type=MESH)

    @pl.when(block > 0)
    def _():
        pl.semaphore_signal(barrier, inc=1, device_id={"ping": block - 1}, device_id_type=MESH)

    @pl.when(block < blocks - 1)
    def _():
        pl.semaphore_signal(barrier, inc=1, device_id={"ping": block + 1}, device_id_type=MESH)

    loads = []
    for k in range(each):
        loads.append([
            pltpu.make_async_copy(staves.at[:, :, k], xbuf.at[k], xsem.at[k]),
            pltpu.make_async_copy(weights.at[:, k], wbuf.at[k], wsem.at[k]),
        ])
        for copy in loads[-1]:
            copy.start()
        if k == 0:
            small = [
                pltpu.make_async_copy(a, b, qsem.at[i])
                for i, (a, b) in enumerate([(replica, qbuf), (start, tbuf.at[0]), (length, tbuf.at[1])])
            ]
            for copy in small:
                copy.start()
    consts = [
        pltpu.make_async_copy(a, b, csem.at[i])
        for i, (a, b) in enumerate([(first_in, first), (twiddle_in, twiddle), (second_in, second), (smooth_in, smooth)])
    ]
    for copy in consts:
        copy.start()

    def across(src, dst, n):
        return pltpu.make_async_remote_copy(
            src, dst, zsend.at[n], zrecv.at[n], device_id=at(y, there_z, r), device_id_type=MESH)

    size = columns * ROW

    def scatter(src, dst, n):
        @pl.loop(1, size)
        def _(i):
            place = lax.rem(mine + i, size)
            pltpu.make_async_remote_copy(
                src.at[place], dst.at[mine], psend.at[n], precv.at[n],
                device_id=at(lax.div(place, ROW), here_z, lax.rem(place, ROW)), device_id_type=MESH,
            ).start()

        dst[mine] = src[mine]

    def scattered(src, dst, n):
        rest = pl.ds(0, size - 1)
        return pltpu.make_async_remote_copy(
            src.at[rest], dst.at[rest], psend.at[n], precv.at[n],
            device_id=at(y, here_z, lax.rem(r + 1, ROW)), device_id_type=MESH)

    sides = (block > 0).astype(jnp.int32) + (block < blocks - 1).astype(jnp.int32)

    def beside(src, dst, up_sems, down_sems):
        up = pltpu.make_async_remote_copy(
            src, dst.at[0], up_sems.at[0], down_sems.at[0], device_id={"ping": block + 1}, device_id_type=MESH)
        down = pltpu.make_async_remote_copy(
            src, dst.at[1], up_sems.at[1], down_sems.at[1], device_id={"ping": block - 1}, device_id_type=MESH)
        return up, down

    def send(copies):
        @pl.when(block < blocks - 1)
        def _():
            copies[0].start()

        @pl.when(block > 0)
        def _():
            copies[1].start()

    def receive(copies):
        @pl.when(block > 0)
        def _():
            copies[0].wait_recv()

        @pl.when(block < blocks - 1)
        def _():
            copies[1].wait_recv()

    def sent(copies):
        @pl.when(block < blocks - 1)
        def _():
            copies[0].wait_send()

        @pl.when(block > 0)
        def _():
            copies[1].wait_send()

    edges = beside(win, near, nsem, msem)

    for copy in small:
        copy.wait()
    span = each * BINS
    spread = functools.partial(jnp.dot, precision=lax.Precision.HIGHEST, preferred_element_type=jnp.float32)
    row, column = (lax.broadcasted_iota(jnp.int32, (128, 128), d) for d in (0, 1))
    per_tile = 128 // span
    part = qbuf[:, pl.ds(pl.multiple_of(lax.div(me, per_tile) * 128, 128), 128)]
    for k in range(each):
        pick = jnp.where(row == lax.rem(me, per_tile) * span + k * BINS + lax.rem(column, BINS), 1.0, 0.0)
        rep[k] = spread(part, pick)
    row, column = (lax.broadcasted_iota(jnp.int32, (16, 128), d) for d in (0, 1))
    pick = jnp.where(row == lax.div(column, BINS), 1.0, 0.0)
    times = spread(tbuf[...].astype(jnp.float32).reshape(16, 16), pick)
    low = times[:8] - (lax.rem(column[:8], BINS) * SPLIT).astype(jnp.float32)
    win[0:8] = low
    win[8:16] = low + times[8:]

    def beams(k, c):
        x = xbuf[k].astype(jnp.float32).reshape(2 * 128, -1).astype(jnp.bfloat16)
        r0, r1 = rep[k, 0:1, :], rep[k, 1:2, :]
        here = pl.ds(c * 256, 256)
        p0 = jnp.dot(x, wbuf[k, 0, :, here], preferred_element_type=jnp.float32)
        p1 = jnp.dot(x, wbuf[k, 1, :, here], preferred_element_type=jnp.float32)
        re = (p0[:128] - p1[128:]).astype(jnp.bfloat16).T.astype(jnp.float32)
        im = (p1[:128] + p0[128:]).astype(jnp.bfloat16).T.astype(jnp.float32)
        return (re * r0 + im * r1).reshape(32, 8, 128), (im * r0 - re * r1).reshape(32, 8, 128)

    def put(n, c, parts):
        tiles = jnp.concatenate(parts, axis=1).astype(jnp.bfloat16)
        for i in range(4):
            sbuf[n, i % 2, (c * 2 + i // 2) * ROW : (c * 2 + i // 2 + 1) * ROW] = tiles[i * ROW : (i + 1) * ROW]

    chunks = wbuf.shape[-1] // 256

    def early(k):
        for copy in loads[k]:
            copy.wait()
        for c in range(chunks):
            put(k, c, beams(k, c))

    early(0)
    pl.semaphore_wait(barrier, size + sides)
    across(sbuf.at[0, there_z], over.at[0], 0).start()
    send(edges)
    for k in (2, 3):
        for copy in loads[k]:
            copy.wait()
    for c in range(chunks):
        a, b = beams(2, c), beams(3, c)
        for h in range(2):
            part = slice(4 * h, 4 * h + 4)
            put(2 + h, c, [a[0][:, part], b[0][:, part], a[1][:, part], b[1][:, part]])
    for h in range(2):
        scatter(sbuf.at[2 + h, there_z], gathered.at[h], 4 + h)
    early(1)
    across(sbuf.at[1, there_z], over.at[1], 1).start()

    scattered(sbuf.at[2, there_z], gathered.at[0], 4).wait_recv()
    across(gathered.at[0], beyond.at[2], 2).start()
    for n in range(3):
        scatter(sbuf.at[n, here_z], plane.at[n], n)
    across(sbuf.at[0, there_z], over.at[0], 0).wait_recv()
    scatter(over.at[0], beyond.at[0], 6)
    scatter(sbuf.at[3, here_z], plane.at[3], 3)
    scattered(sbuf.at[3, there_z], gathered.at[1], 5).wait_recv()
    across(sbuf.at[1, there_z], over.at[1], 1).wait_recv()
    across(gathered.at[1], beyond.at[3], 3).start()
    scatter(over.at[1], beyond.at[1], 7)

    half = columns * ROW * 16

    def unpack(n, slot, tiles):
        fbuf[n, slot] = tiles.astype(jnp.float32).reshape(half, 128)

    for copy in consts:
        copy.wait()
    receive(edges)
    lane = lax.broadcasted_iota(jnp.int32, (16, 128), 1)
    wide = jnp.where(lane < 8 * REACH, near[1], jnp.where(lane >= 128 - 8 * REACH, near[0], 4096.0))
    near[0] = wide
    rows = lax.broadcasted_iota(jnp.int32, (SPLIT, 1), 0).astype(jnp.float32)

    for k in range(2):
        scattered(sbuf.at[k, here_z], plane.at[k], k).wait_recv()
        unpack(k, 0, plane[k])
        scattered(over.at[k], beyond.at[k], 6 + k).wait_recv()
        unpack(k, 1, beyond[k])

    def window(b, g):
        sm = jnp.dot(ebuf[b], smooth[:, g * 128 : (g + 1) * 128], preferred_element_type=jnp.float32)
        source = win if g == 0 else near.at[0]
        low, high = source[pl.ds(b, 1), :], source[pl.ds(b + 8, 1), :]
        v = jnp.where((rows >= low) & (rows < high), sm, 0.0)
        e = jnp.sum(v, axis=0, keepdims=True)
        m = jnp.sum(v * rows, axis=0, keepdims=True) + (0.5 - low) * e
        acc[g, pl.ds(b, 1), :] = e
        acc[g, pl.ds(b + 8, 1), :] = m

    def gather(half_of, pair, slot, late):
        base = (slot * 2 + late) * 2 * 2 * size
        for i in range(2):
            for j in range(2):
                for h in range(2):
                    q = pair * 2 + h
                    n, at_row = (2 + half_of, j * 4 + q) if late else (j, half_of * 4 + q)
                    part = fbuf[n, slot, pl.ds(i * 8 + at_row, size, stride=16), :]
                    rhs[pair, pl.ds(base + (i * 2 + j) * size, size), h * 128 : (h + 1) * 128] = part.astype(jnp.bfloat16)

    def prepare(half_of, pair):
        for slot, late in ((0, 0), (0, 1), (1, 0)):
            gather(half_of, pair, slot, late)
        span = 8 * size
        sums[pair] = jnp.dot(first[here_z], rhs[pair, :span], preferred_element_type=jnp.float32) + jnp.dot(
            first[there_z, :, : span // 2], rhs[pair, span : span * 3 // 2], preferred_element_type=jnp.float32)

    def transform(half_of, pair):
        gather(half_of, pair, 1, 1)
        span = 8 * size
        out = sums[pair] + jnp.dot(
            first[there_z, :, span // 2 :], rhs[pair, span * 3 // 2 :], preferred_element_type=jnp.float32)
        for h in range(2):
            re, im = out[:SPLIT, h * 128 : (h + 1) * 128], out[SPLIT:, h * 128 : (h + 1) * 128]
            c, s = twiddle[0], twiddle[1]
            z = jnp.concatenate([re * c - im * s, re * s + im * c], axis=1).astype(jnp.bfloat16)
            w = jnp.dot(z, second[...], preferred_element_type=jnp.float32)
            wr, wi = w[:, :128], w[:, 128:]
            ebuf[half_of * 4 + pair * 2 + h] = (wr * wr + wi * wi).astype(jnp.bfloat16)
            window(half_of * 4 + pair * 2 + h, 1)

    partial = beside(acc.at[1], hrecv, hsem, gsem)
    for h in range(2):
        scattered(sbuf.at[2 + h, here_z], plane.at[2 + h], 2 + h).wait_recv()
        unpack(2 + h, 0, plane[2 + h])
        for pair in range(2):
            prepare(h, pair)
        across(gathered.at[h], beyond.at[2 + h], 2 + h).wait_recv()
        unpack(2 + h, 1, beyond[2 + h])
        for pair in range(2):
            transform(h, pair)

        if h == 1:
            send(partial)

        for q in range(4):
            window(h * 4 + q, 0)

    receive(partial)
    total = acc[0] + jnp.where(lane < 8 * REACH, hrecv[0], 0.0) + jnp.where(lane >= 128 - 8 * REACH, hrecv[1], 0.0)
    rowp = lax.broadcasted_iota(jnp.int32, (16, 128), 0)
    group = jnp.where(lane // 8 == rowp, 1.0, 0.0)
    both = lax.dot_general(
        total, group, (((1,), (1,)), ((), ())), precision=lax.Precision.HIGHEST, preferred_element_type=jnp.float32)
    place = block * 16 + lax.broadcasted_iota(jnp.int32, (8, 16), 1)
    weight = jnp.zeros((8, 16), jnp.float32)
    for j, tap in enumerate(TAPS):
        q = place + (j - REACH)
        weight = weight + jnp.where((q >= 0) & (q < blocks * 16), tap, 0.0)
    scale = (1.0 / (16.0 * SPLIT * BINS)) / weight
    e, m = both[:8] * scale, both[8:] * scale
    widths = tbuf[1].astype(jnp.float32)
    result[0] = m / (widths * (e + 1e-06))
    result[1] = e / widths

    sent(edges)
    sent(partial)
    for k in range(2):
        scattered(sbuf.at[k, here_z], plane.at[k], k).wait_send()
        scattered(sbuf.at[2 + k, here_z], plane.at[2 + k], 2 + k).wait_send()
        scattered(sbuf.at[2 + k, there_z], gathered.at[k], 4 + k).wait_send()
        scattered(over.at[k], beyond.at[k], 6 + k).wait_send()
        across(sbuf.at[k, there_z], over.at[k], k).wait_send()
        across(gathered.at[k], beyond.at[2 + k], 2 + k).wait_send()


def local(bands, blocks, staves, weights, replica, start, length):
    each = weights.shape[1]
    first, twiddle, second, smooth = tables(bands, each)
    vmem, hbm = pl.BlockSpec(memory_space=pltpu.VMEM), pl.BlockSpec(memory_space=pltpu.HBM)
    f32, bf16, dma = jnp.float32, jnp.bfloat16, pltpu.SemaphoreType.DMA
    plane = (bands // 2, 16, 128)
    out = pl.pallas_call(
        functools.partial(kernel, bands, blocks),
        out_shape=jax.ShapeDtypeStruct((2, 8, 16), f32),
        in_specs=[hbm] * 9,
        out_specs=vmem,
        scratch_shapes=[
            pltpu.VMEM(replica.shape, f32),
            pltpu.VMEM((2, 8, 16), jnp.int32),
            pltpu.VMEM((each, 2, 128), f32),
            pltpu.VMEM((16, 128), f32),
            pltpu.VMEM((each, 2, 16, 8, 512), bf16),
            pltpu.VMEM((each, 2, 512, 512), bf16),
            pltpu.VMEM((each, 2, *plane), bf16),
            pltpu.VMEM((2, *plane), bf16),
            pltpu.VMEM((2, *plane), bf16),
            pltpu.VMEM((each, *plane), bf16),
            pltpu.VMEM((each, *plane), bf16),
            pltpu.VMEM((each, 2, bands * 8, 128), f32),
            pltpu.VMEM((2, 2 * each * bands, 256), bf16),
            pltpu.VMEM((2, 2 * SPLIT, 256), f32),
            pltpu.VMEM((8, SPLIT, 128), bf16),
            pltpu.VMEM(first.shape, bf16),
            pltpu.VMEM(twiddle.shape, f32),
            pltpu.VMEM(second.shape, bf16),
            pltpu.VMEM(smooth.shape, bf16),
            pltpu.VMEM((2, 16, 128), f32),
            pltpu.VMEM((2, 16, 128), f32),
            pltpu.VMEM((2, 16, 128), f32),
            dma((3,)), dma((each,)), dma((each,)), dma((4,)),
            dma((8,)), dma((8,)), dma((each,)), dma((each,)),
            dma((2,)), dma((2,)), dma((2,)), dma((2,)),
        ],
        compiler_params=pltpu.CompilerParams(collective_id=0, has_side_effects=True, vmem_limit_bytes=63 << 20),
    )(staves, weights, replica, start.T, length.T, first, twiddle, second, smooth)
    return out[0].T, out[1].T


def solution(mesh):
    in_specs = (
        P(None, "ping", "band", None, None),
        P(None, "band", None, None),
        P(),
        P("ping", "band"),
        P("ping", "band"),
    )
    out_specs = (P("ping", "band"), P("ping", "band"))
    step = functools.partial(local, mesh.shape["band"], mesh.shape["ping"])
    return jax.shard_map(step, mesh=mesh, in_specs=in_specs, out_specs=out_specs, check_vma=False)
```

```python
import functools
import math

import ml_dtypes
import numpy as np

import jax
import jax.numpy as jnp
from jax import lax
from jax.experimental import pallas as pl
from jax.experimental.pallas import tpu as pltpu
from jax.sharding import PartitionSpec as P

MESH = pl.DeviceIdType.MESH
BINS, SPLIT, REACH = 8, 256, 4
ROW = 8
TAPS = (1.0, 2.0, 3.0, 4.0, 5.0, 4.0, 3.0, 2.0, 1.0)


def tables(sources, bands_each):
    total = SPLIT * BINS
    turn = 2.0 * math.pi / total
    t1 = np.arange(SPLIT)
    place = np.arange(sources // 2)
    first = []
    for z in range(2):
        source = (place // ROW * 2 + z) * ROW + place % ROW
        columns = []
        for pair in range(bands_each // 2):
            band = (source[None, :] * bands_each + pair * 2 + np.arange(2)[:, None]).reshape(-1)
            angle = ((t1[:, None] * band[None, :] * BINS) % total) * turn
            cos, sin = np.cos(angle), np.sin(angle)
            columns.append(np.block([[cos, -sin], [sin, cos]]))
        first.append(np.concatenate(columns, axis=1))
    first = np.stack(first)
    lane = np.arange(128)
    ping, small = lane // BINS, lane % BINS
    angle = ((t1[:, None] * small[None, :]) % total) * turn
    twiddle = np.stack([np.cos(angle), np.sin(angle)])
    same = ping[:, None] == ping[None, :]
    angle = ((small[:, None] * small[None, :]) % BINS) * (2.0 * math.pi / BINS)
    cos, sin = np.cos(angle) * same, np.sin(angle) * same
    second = np.block([[cos, sin], [-sin, cos]])
    above, below = ping + 16, ping - 16
    beside = np.where(ping < REACH, above, np.where(ping >= 16 - REACH, below, 1000))
    target = np.concatenate([ping, beside])
    kind = np.concatenate([small, small])
    smooth = np.maximum(5 - np.abs(ping[:, None] - target[None, :]), 0) * (small[:, None] == kind[None, :])
    half = ml_dtypes.bfloat16
    return first.astype(half), twiddle.astype(np.float32), second.astype(half), smooth.astype(half)


def kernel(
    bands, blocks,
    staves, weights, replica, start, length, first_in, twiddle_in, second_in, smooth_in,
    result,
    qbuf, tbuf, rep, win, xbuf, wbuf, sbuf, over, gathered, plane, beyond, fbuf, rhs, sums, ebuf,
    first, twiddle, second, smooth, near, acc, hrecv,
    qsem, xsem, wsem, csem, psend, precv, zsend, zrecv, nsem, msem, hsem, gsem, met,
):
    me, block = lax.axis_index("band"), lax.axis_index("ping")
    each = wbuf.shape[0]
    columns = bands // (2 * ROW)
    here_z = lax.rem(lax.div(me, ROW), 2)
    there_z = 1 - here_z
    y, r = lax.div(me, 2 * ROW), lax.rem(me, ROW)
    mine = y * ROW + r

    def at(y, z, r):
        return {"band": (y * 2 + z) * ROW + r}

    near[...] = jnp.zeros_like(near)
    hrecv[...] = jnp.zeros_like(hrecv)

    barrier = pltpu.get_barrier_semaphore()
    pl.semaphore_signal(barrier, inc=1, device_id=at(y, there_z, r), device_id_type=MESH)

    def along(step):
        place = lax.rem(mine + step + columns * ROW, columns * ROW)
        return at(lax.div(place, ROW), here_z, lax.rem(place, ROW))

    for step in (1, -1, 2, -2):
        pl.semaphore_signal(barrier, inc=1, device_id=along(step), device_id_type=MESH)

    @pl.when(block > 0)
    def _():
        pl.semaphore_signal(barrier, inc=1, device_id={"ping": block - 1}, device_id_type=MESH)

    @pl.when(block < blocks - 1)
    def _():
        pl.semaphore_signal(barrier, inc=1, device_id={"ping": block + 1}, device_id_type=MESH)

    loads = []
    for k in range(each):
        loads.append([
            pltpu.make_async_copy(staves.at[:, :, k], xbuf.at[k], xsem.at[k]),
            pltpu.make_async_copy(weights.at[:, k], wbuf.at[k], wsem.at[k]),
        ])
        for copy in loads[-1]:
            copy.start()
        if k == 0:
            small = [
                pltpu.make_async_copy(a, b, qsem.at[i])
                for i, (a, b) in enumerate([(replica, qbuf), (start, tbuf.at[0]), (length, tbuf.at[1])])
            ]
            for copy in small:
                copy.start()
    consts = [
        pltpu.make_async_copy(a, b, csem.at[i])
        for i, (a, b) in enumerate([(first_in, first), (twiddle_in, twiddle), (second_in, second), (smooth_in, smooth)])
    ]
    for copy in consts:
        copy.start()

    def across(src, dst, n):
        return pltpu.make_async_remote_copy(
            src, dst, zsend.at[n], zrecv.at[n], device_id=at(y, there_z, r), device_id_type=MESH)

    size = columns * ROW

    def scatter(src, dst, n):
        @pl.loop(1, size)
        def _(i):
            place = lax.rem(mine + i, size)
            pltpu.make_async_remote_copy(
                src.at[place], dst.at[mine], psend.at[n], precv.at[n],
                device_id=at(lax.div(place, ROW), here_z, lax.rem(place, ROW)), device_id_type=MESH,
            ).start()

        dst[mine] = src[mine]

    def scattered(src, dst, n):
        rest = pl.ds(0, size - 1)
        return pltpu.make_async_remote_copy(
            src.at[rest], dst.at[rest], psend.at[n], precv.at[n],
            device_id=at(y, here_z, lax.rem(r + 1, ROW)), device_id_type=MESH)

    sides = (block > 0).astype(jnp.int32) + (block < blocks - 1).astype(jnp.int32)

    def beside(src, dst, up_sems, down_sems):
        up = pltpu.make_async_remote_copy(
            src, dst.at[0], up_sems.at[0], down_sems.at[0], device_id={"ping": block + 1}, device_id_type=MESH)
        down = pltpu.make_async_remote_copy(
            src, dst.at[1], up_sems.at[1], down_sems.at[1], device_id={"ping": block - 1}, device_id_type=MESH)
        return up, down

    def send(copies):
        @pl.when(block < blocks - 1)
        def _():
            copies[0].start()

        @pl.when(block > 0)
        def _():
            copies[1].start()

    def receive(copies):
        @pl.when(block > 0)
        def _():
            copies[0].wait_recv()

        @pl.when(block < blocks - 1)
        def _():
            copies[1].wait_recv()

    def sent(copies):
        @pl.when(block < blocks - 1)
        def _():
            copies[0].wait_send()

        @pl.when(block > 0)
        def _():
            copies[1].wait_send()

    edges = beside(win, near, nsem, msem)

    for copy in small:
        copy.wait()
    span = each * BINS
    spread = functools.partial(jnp.dot, precision=lax.Precision.HIGHEST, preferred_element_type=jnp.float32)
    row, column = (lax.broadcasted_iota(jnp.int32, (128, 128), d) for d in (0, 1))
    per_tile = 128 // span
    part = qbuf[:, pl.ds(pl.multiple_of(lax.div(me, per_tile) * 128, 128), 128)]
    for k in range(each):
        pick = jnp.where(row == lax.rem(me, per_tile) * span + k * BINS + lax.rem(column, BINS), 1.0, 0.0)
        rep[k] = spread(part, pick)
    row, column = (lax.broadcasted_iota(jnp.int32, (16, 128), d) for d in (0, 1))
    pick = jnp.where(row == lax.div(column, BINS), 1.0, 0.0)
    times = spread(tbuf[...].astype(jnp.float32).reshape(16, 16), pick)
    low = times[:8] - (lax.rem(column[:8], BINS) * SPLIT).astype(jnp.float32)
    win[0:8] = low
    win[8:16] = low + times[8:]

    def tell(turn):
        for side in range(2):
            pl.semaphore_signal(
                met.at[turn, side], inc=1, device_id=along((2 << turn) * (1 - 2 * side)), device_id_type=MESH)

    def hear(turn):
        for side in range(2):
            pl.semaphore_wait(met.at[turn, side], 1)

    def beams(k, c):
        x = xbuf[k].astype(jnp.float32).reshape(2 * 128, -1).astype(jnp.bfloat16)
        r0, r1 = rep[k, 0:1, :], rep[k, 1:2, :]
        here = pl.ds(c * 256, 256)
        p0 = jnp.dot(x, wbuf[k, 0, :, here], preferred_element_type=jnp.float32)
        p1 = jnp.dot(x, wbuf[k, 1, :, here], preferred_element_type=jnp.float32)
        re = (p0[:128] - p1[128:]).astype(jnp.bfloat16).T.astype(jnp.float32)
        im = (p1[:128] + p0[128:]).astype(jnp.bfloat16).T.astype(jnp.float32)
        return (re * r0 + im * r1).reshape(32, 8, 128), (im * r0 - re * r1).reshape(32, 8, 128)

    def put(n, c, parts):
        tiles = jnp.concatenate(parts, axis=1).astype(jnp.bfloat16)
        for i in range(4):
            sbuf[n, i % 2, (c * 2 + i // 2) * ROW : (c * 2 + i // 2 + 1) * ROW] = tiles[i * ROW : (i + 1) * ROW]

    chunks = wbuf.shape[-1] // 256

    def early(k):
        for copy in loads[k]:
            copy.wait()
        for c in range(chunks):
            put(k, c, beams(k, c))

    early(0)
    pl.semaphore_wait(barrier, 5 + sides)
    tell(0)
    across(sbuf.at[0, there_z], over.at[0], 0).start()
    send(edges)
    early(1)
    across(sbuf.at[1, there_z], over.at[1], 1).start()
    hear(0)
    tell(1)
    for k in (2, 3):
        for copy in loads[k]:
            copy.wait()
    for c in range(chunks):
        a, b = beams(2, c), beams(3, c)
        for h in range(2):
            part = slice(4 * h, 4 * h + 4)
            put(2 + h, c, [a[0][:, part], b[0][:, part], a[1][:, part], b[1][:, part]])
        hear(1 + c)
        if c == 0:
            tell(2)
    for h in range(2):
        scatter(sbuf.at[2 + h, there_z], gathered.at[h], 4 + h)
    scattered(sbuf.at[2, there_z], gathered.at[0], 4).wait_recv()
    across(gathered.at[0], beyond.at[2], 2).start()
    for n in range(3):
        scatter(sbuf.at[n, here_z], plane.at[n], n)
    across(sbuf.at[0, there_z], over.at[0], 0).wait_recv()
    scatter(over.at[0], beyond.at[0], 6)
    scatter(sbuf.at[3, here_z], plane.at[3], 3)
    scattered(sbuf.at[3, there_z], gathered.at[1], 5).wait_recv()
    across(sbuf.at[1, there_z], over.at[1], 1).wait_recv()
    across(gathered.at[1], beyond.at[3], 3).start()
    scatter(over.at[1], beyond.at[1], 7)

    half = columns * ROW * 16

    def unpack(n, slot, tiles):
        fbuf[n, slot] = tiles.astype(jnp.float32).reshape(half, 128)

    for copy in consts:
        copy.wait()
    receive(edges)
    lane = lax.broadcasted_iota(jnp.int32, (16, 128), 1)
    wide = jnp.where(lane < 8 * REACH, near[1], jnp.where(lane >= 128 - 8 * REACH, near[0], 4096.0))
    near[0] = wide
    rows = lax.broadcasted_iota(jnp.int32, (SPLIT, 1), 0).astype(jnp.float32)

    for k in range(2):
        scattered(sbuf.at[k, here_z], plane.at[k], k).wait_recv()
        unpack(k, 0, plane[k])
        scattered(over.at[k], beyond.at[k], 6 + k).wait_recv()
        unpack(k, 1, beyond[k])

    def window(b, g):
        sm = jnp.dot(ebuf[b], smooth[:, g * 128 : (g + 1) * 128], preferred_element_type=jnp.float32)
        source = win if g == 0 else near.at[0]
        low, high = source[pl.ds(b, 1), :], source[pl.ds(b + 8, 1), :]
        v = jnp.where((rows >= low) & (rows < high), sm, 0.0)
        e = jnp.sum(v, axis=0, keepdims=True)
        m = jnp.sum(v * rows, axis=0, keepdims=True) + (0.5 - low) * e
        acc[g, pl.ds(b, 1), :] = e
        acc[g, pl.ds(b + 8, 1), :] = m

    def gather(half_of, pair, slot, late):
        base = (slot * 2 + late) * 2 * 2 * size
        for i in range(2):
            for j in range(2):
                for h in range(2):
                    q = pair * 2 + h
                    n, at_row = (2 + half_of, j * 4 + q) if late else (j, half_of * 4 + q)
                    part = fbuf[n, slot, pl.ds(i * 8 + at_row, size, stride=16), :]
                    rhs[pair, pl.ds(base + (i * 2 + j) * size, size), h * 128 : (h + 1) * 128] = part.astype(jnp.bfloat16)

    def prepare(half_of, pair):
        for slot, late in ((0, 0), (0, 1), (1, 0)):
            gather(half_of, pair, slot, late)
        span = 8 * size
        sums[pair] = jnp.dot(first[here_z], rhs[pair, :span], preferred_element_type=jnp.float32) + jnp.dot(
            first[there_z, :, : span // 2], rhs[pair, span : span * 3 // 2], preferred_element_type=jnp.float32)

    def transform(half_of, pair):
        gather(half_of, pair, 1, 1)
        span = 8 * size
        out = sums[pair] + jnp.dot(
            first[there_z, :, span // 2 :], rhs[pair, span * 3 // 2 :], preferred_element_type=jnp.float32)
        for h in range(2):
            re, im = out[:SPLIT, h * 128 : (h + 1) * 128], out[SPLIT:, h * 128 : (h + 1) * 128]
            c, s = twiddle[0], twiddle[1]
            z = jnp.concatenate([re * c - im * s, re * s + im * c], axis=1).astype(jnp.bfloat16)
            w = jnp.dot(z, second[...], preferred_element_type=jnp.float32)
            wr, wi = w[:, :128], w[:, 128:]
            ebuf[half_of * 4 + pair * 2 + h] = (wr * wr + wi * wi).astype(jnp.bfloat16)
            window(half_of * 4 + pair * 2 + h, 1)

    partial = beside(acc.at[1], hrecv, hsem, gsem)
    for h in range(2):
        scattered(sbuf.at[2 + h, here_z], plane.at[2 + h], 2 + h).wait_recv()
        unpack(2 + h, 0, plane[2 + h])
        for pair in range(2):
            prepare(h, pair)
        across(gathered.at[h], beyond.at[2 + h], 2 + h).wait_recv()
        unpack(2 + h, 1, beyond[2 + h])
        for pair in range(2):
            transform(h, pair)

        if h == 1:
            send(partial)

        for q in range(4):
            window(h * 4 + q, 0)

    receive(partial)
    total = acc[0] + jnp.where(lane < 8 * REACH, hrecv[0], 0.0) + jnp.where(lane >= 128 - 8 * REACH, hrecv[1], 0.0)
    rowp = lax.broadcasted_iota(jnp.int32, (16, 128), 0)
    group = jnp.where(lane // 8 == rowp, 1.0, 0.0)
    both = lax.dot_general(
        total, group, (((1,), (1,)), ((), ())), precision=lax.Precision.HIGHEST, preferred_element_type=jnp.float32)
    place = block * 16 + lax.broadcasted_iota(jnp.int32, (8, 16), 1)
    weight = jnp.zeros((8, 16), jnp.float32)
    for j, tap in enumerate(TAPS):
        q = place + (j - REACH)
        weight = weight + jnp.where((q >= 0) & (q < blocks * 16), tap, 0.0)
    scale = (1.0 / (16.0 * SPLIT * BINS)) / weight
    e, m = both[:8] * scale, both[8:] * scale
    widths = tbuf[1].astype(jnp.float32)
    result[0] = m / (widths * (e + 1e-06))
    result[1] = e / widths

    sent(edges)
    sent(partial)
    for k in range(2):
        scattered(sbuf.at[k, here_z], plane.at[k], k).wait_send()
        scattered(sbuf.at[2 + k, here_z], plane.at[2 + k], 2 + k).wait_send()
        scattered(sbuf.at[2 + k, there_z], gathered.at[k], 4 + k).wait_send()
        scattered(over.at[k], beyond.at[k], 6 + k).wait_send()
        across(sbuf.at[k, there_z], over.at[k], k).wait_send()
        across(gathered.at[k], beyond.at[2 + k], 2 + k).wait_send()


def local(bands, blocks, staves, weights, replica, start, length):
    each = weights.shape[1]
    first, twiddle, second, smooth = tables(bands, each)
    vmem, hbm = pl.BlockSpec(memory_space=pltpu.VMEM), pl.BlockSpec(memory_space=pltpu.HBM)
    f32, bf16, dma = jnp.float32, jnp.bfloat16, pltpu.SemaphoreType.DMA
    plane = (bands // 2, 16, 128)
    out = pl.pallas_call(
        functools.partial(kernel, bands, blocks),
        out_shape=jax.ShapeDtypeStruct((2, 8, 16), f32),
        in_specs=[hbm] * 9,
        out_specs=vmem,
        scratch_shapes=[
            pltpu.VMEM(replica.shape, f32),
            pltpu.VMEM((2, 8, 16), jnp.int32),
            pltpu.VMEM((each, 2, 128), f32),
            pltpu.VMEM((16, 128), f32),
            pltpu.VMEM((each, 2, 16, 8, 512), bf16),
            pltpu.VMEM((each, 2, 512, 512), bf16),
            pltpu.VMEM((each, 2, *plane), bf16),
            pltpu.VMEM((2, *plane), bf16),
            pltpu.VMEM((2, *plane), bf16),
            pltpu.VMEM((each, *plane), bf16),
            pltpu.VMEM((each, *plane), bf16),
            pltpu.VMEM((each, 2, bands * 8, 128), f32),
            pltpu.VMEM((2, 2 * each * bands, 256), bf16),
            pltpu.VMEM((2, 2 * SPLIT, 256), f32),
            pltpu.VMEM((8, SPLIT, 128), bf16),
            pltpu.VMEM(first.shape, bf16),
            pltpu.VMEM(twiddle.shape, f32),
            pltpu.VMEM(second.shape, bf16),
            pltpu.VMEM(smooth.shape, bf16),
            pltpu.VMEM((2, 16, 128), f32),
            pltpu.VMEM((2, 16, 128), f32),
            pltpu.VMEM((2, 16, 128), f32),
            dma((3,)), dma((each,)), dma((each,)), dma((4,)),
            dma((8,)), dma((8,)), dma((each,)), dma((each,)),
            dma((2,)), dma((2,)), dma((2,)), dma((2,)),
            pltpu.SemaphoreType.REGULAR((3, 2)),
        ],
        compiler_params=pltpu.CompilerParams(collective_id=0, has_side_effects=True, vmem_limit_bytes=63 << 20),
    )(staves, weights, replica, start.T, length.T, first, twiddle, second, smooth)
    return out[0].T, out[1].T


def solution(mesh):
    in_specs = (
        P(None, "ping", "band", None, None),
        P(None, "band", None, None),
        P(),
        P("ping", "band"),
        P("ping", "band"),
    )
    out_specs = (P("ping", "band"), P("ping", "band"))
    step = functools.partial(local, mesh.shape["band"], mesh.shape["ping"])
    return jax.shard_map(step, mesh=mesh, in_specs=in_specs, out_specs=out_specs, check_vma=False)
```

```python
import functools
import math

import ml_dtypes
import numpy as np

import jax
import jax.numpy as jnp
from jax import lax
from jax.experimental import pallas as pl
from jax.experimental.pallas import tpu as pltpu
from jax.sharding import PartitionSpec as P

MESH = pl.DeviceIdType.MESH
BINS, SPLIT, REACH = 8, 256, 4
ROW = 8
TAPS = (1.0, 2.0, 3.0, 4.0, 5.0, 4.0, 3.0, 2.0, 1.0)


def tables(sources, bands_each):
    total = SPLIT * BINS
    turn = 2.0 * math.pi / total
    t1 = np.arange(SPLIT)
    place = np.arange(sources // 2)
    first = []
    for z in range(2):
        source = (place // ROW * 2 + z) * ROW + place % ROW
        columns = []
        for pair in range(bands_each // 2):
            band = (source[None, :] * bands_each + pair * 2 + np.arange(2)[:, None]).reshape(-1)
            angle = ((t1[:, None] * band[None, :] * BINS) % total) * turn
            cos, sin = np.cos(angle), np.sin(angle)
            columns.append(np.block([[cos, -sin], [sin, cos]]))
        first.append(np.concatenate(columns, axis=1))
    first = np.stack(first)
    lane = np.arange(128)
    ping, small = lane // BINS, lane % BINS
    angle = ((t1[:, None] * small[None, :]) % total) * turn
    twiddle = np.stack([np.cos(angle), np.sin(angle)])
    same = ping[:, None] == ping[None, :]
    angle = ((small[:, None] * small[None, :]) % BINS) * (2.0 * math.pi / BINS)
    cos, sin = np.cos(angle) * same, np.sin(angle) * same
    second = np.block([[cos, sin], [-sin, cos]])
    above, below = ping + 16, ping - 16
    beside = np.where(ping < REACH, above, np.where(ping >= 16 - REACH, below, 1000))
    target = np.concatenate([ping, beside])
    kind = np.concatenate([small, small])
    smooth = np.maximum(5 - np.abs(ping[:, None] - target[None, :]), 0) * (small[:, None] == kind[None, :])
    half = ml_dtypes.bfloat16
    return first.astype(half), twiddle.astype(np.float32), second.astype(half), smooth.astype(half)


def kernel(
    bands, blocks,
    staves, weights, replica, start, length, first_in, twiddle_in, second_in, smooth_in,
    result,
    qbuf, tbuf, rep, win, xbuf, wbuf, sbuf, over, gathered, plane, beyond, fbuf, rhs, sums, ebuf,
    first, twiddle, second, smooth, near, acc, hrecv,
    qsem, xsem, wsem, csem, psend, precv, zsend, zrecv, nsem, msem, hsem, gsem, met,
):
    me, block = lax.axis_index("band"), lax.axis_index("ping")
    each = wbuf.shape[0]
    columns = bands // (2 * ROW)
    here_z = lax.rem(lax.div(me, ROW), 2)
    there_z = 1 - here_z
    y, r = lax.div(me, 2 * ROW), lax.rem(me, ROW)
    mine = y * ROW + r

    def at(y, z, r):
        return {"band": (y * 2 + z) * ROW + r}

    near[...] = jnp.zeros_like(near)
    hrecv[...] = jnp.zeros_like(hrecv)

    barrier = pltpu.get_barrier_semaphore()
    pl.semaphore_signal(barrier, inc=1, device_id=at(y, there_z, r), device_id_type=MESH)

    def along(step):
        place = lax.rem(mine + step + columns * ROW, columns * ROW)
        return at(lax.div(place, ROW), here_z, lax.rem(place, ROW))

    for step in (1, -1, 2, -2, 3, -3, 4, -4):
        pl.semaphore_signal(barrier, inc=1, device_id=along(step), device_id_type=MESH)

    @pl.when(block > 0)
    def _():
        pl.semaphore_signal(barrier, inc=1, device_id={"ping": block - 1}, device_id_type=MESH)

    @pl.when(block < blocks - 1)
    def _():
        pl.semaphore_signal(barrier, inc=1, device_id={"ping": block + 1}, device_id_type=MESH)

    loads = []
    for k in range(each):
        loads.append([
            pltpu.make_async_copy(staves.at[:, :, k], xbuf.at[k], xsem.at[k]),
            pltpu.make_async_copy(weights.at[:, k], wbuf.at[k], wsem.at[k]),
        ])
        for copy in loads[-1]:
            copy.start()
        if k == 0:
            small = [
                pltpu.make_async_copy(a, b, qsem.at[i])
                for i, (a, b) in enumerate([(replica, qbuf), (start, tbuf.at[0]), (length, tbuf.at[1])])
            ]
            for copy in small:
                copy.start()
    consts = [
        pltpu.make_async_copy(a, b, csem.at[i])
        for i, (a, b) in enumerate([(first_in, first), (twiddle_in, twiddle), (second_in, second), (smooth_in, smooth)])
    ]
    for copy in consts:
        copy.start()

    def across(src, dst, n):
        return pltpu.make_async_remote_copy(
            src, dst, zsend.at[n], zrecv.at[n], device_id=at(y, there_z, r), device_id_type=MESH)

    size = columns * ROW

    def scatter(src, dst, n):
        @pl.loop(1, size)
        def _(i):
            place = lax.rem(mine + i, size)
            pltpu.make_async_remote_copy(
                src.at[place], dst.at[mine], psend.at[n], precv.at[n],
                device_id=at(lax.div(place, ROW), here_z, lax.rem(place, ROW)), device_id_type=MESH,
            ).start()

        dst[mine] = src[mine]

    def scattered(src, dst, n):
        rest = pl.ds(0, size - 1)
        return pltpu.make_async_remote_copy(
            src.at[rest], dst.at[rest], psend.at[n], precv.at[n],
            device_id=at(y, here_z, lax.rem(r + 1, ROW)), device_id_type=MESH)

    sides = (block > 0).astype(jnp.int32) + (block < blocks - 1).astype(jnp.int32)

    def beside(src, dst, up_sems, down_sems):
        up = pltpu.make_async_remote_copy(
            src, dst.at[0], up_sems.at[0], down_sems.at[0], device_id={"ping": block + 1}, device_id_type=MESH)
        down = pltpu.make_async_remote_copy(
            src, dst.at[1], up_sems.at[1], down_sems.at[1], device_id={"ping": block - 1}, device_id_type=MESH)
        return up, down

    def send(copies):
        @pl.when(block < blocks - 1)
        def _():
            copies[0].start()

        @pl.when(block > 0)
        def _():
            copies[1].start()

    def receive(copies):
        @pl.when(block > 0)
        def _():
            copies[0].wait_recv()

        @pl.when(block < blocks - 1)
        def _():
            copies[1].wait_recv()

    def sent(copies):
        @pl.when(block < blocks - 1)
        def _():
            copies[0].wait_send()

        @pl.when(block > 0)
        def _():
            copies[1].wait_send()

    edges = beside(win, near, nsem, msem)

    for copy in small:
        copy.wait()
    span = each * BINS
    spread = functools.partial(jnp.dot, precision=lax.Precision.HIGHEST, preferred_element_type=jnp.float32)
    row, column = (lax.broadcasted_iota(jnp.int32, (128, 128), d) for d in (0, 1))
    per_tile = 128 // span
    part = qbuf[:, pl.ds(pl.multiple_of(lax.div(me, per_tile) * 128, 128), 128)]
    for k in range(each):
        pick = jnp.where(row == lax.rem(me, per_tile) * span + k * BINS + lax.rem(column, BINS), 1.0, 0.0)
        rep[k] = spread(part, pick)
    row, column = (lax.broadcasted_iota(jnp.int32, (16, 128), d) for d in (0, 1))
    pick = jnp.where(row == lax.div(column, BINS), 1.0, 0.0)
    times = spread(tbuf[...].astype(jnp.float32).reshape(16, 16), pick)
    low = times[:8] - (lax.rem(column[:8], BINS) * SPLIT).astype(jnp.float32)
    win[0:8] = low
    win[8:16] = low + times[8:]

    def tell(turn):
        for side in range(2):
            pl.semaphore_signal(
                met.at[turn, side], inc=1, device_id=along((4 << turn) * (1 - 2 * side)), device_id_type=MESH)

    def hear(turn):
        for side in range(2):
            pl.semaphore_wait(met.at[turn, side], 1)

    def beams(k, c):
        x = xbuf[k].astype(jnp.float32).reshape(2 * 128, -1).astype(jnp.bfloat16)
        r0, r1 = rep[k, 0:1, :], rep[k, 1:2, :]
        here = pl.ds(c * 256, 256)
        p0 = jnp.dot(x, wbuf[k, 0, :, here], preferred_element_type=jnp.float32)
        p1 = jnp.dot(x, wbuf[k, 1, :, here], preferred_element_type=jnp.float32)
        re = (p0[:128] - p1[128:]).astype(jnp.bfloat16).T.astype(jnp.float32)
        im = (p1[:128] + p0[128:]).astype(jnp.bfloat16).T.astype(jnp.float32)
        return (re * r0 + im * r1).reshape(32, 8, 128), (im * r0 - re * r1).reshape(32, 8, 128)

    def put(n, c, parts):
        tiles = jnp.concatenate(parts, axis=1).astype(jnp.bfloat16)
        for i in range(4):
            sbuf[n, i % 2, (c * 2 + i // 2) * ROW : (c * 2 + i // 2 + 1) * ROW] = tiles[i * ROW : (i + 1) * ROW]

    chunks = wbuf.shape[-1] // 256

    def early(k):
        for copy in loads[k]:
            copy.wait()
        for c in range(chunks):
            put(k, c, beams(k, c))

    early(0)
    pl.semaphore_wait(barrier, 9 + sides)
    tell(0)
    across(sbuf.at[0, there_z], over.at[0], 0).start()
    send(edges)
    early(1)
    across(sbuf.at[1, there_z], over.at[1], 1).start()
    hear(0)
    tell(1)
    for k in (2, 3):
        for copy in loads[k]:
            copy.wait()
    for c in range(chunks):
        a, b = beams(2, c), beams(3, c)
        for h in range(2):
            part = slice(4 * h, 4 * h + 4)
            put(2 + h, c, [a[0][:, part], b[0][:, part], a[1][:, part], b[1][:, part]])
    hear(1)
    for h in range(2):
        scatter(sbuf.at[2 + h, there_z], gathered.at[h], 4 + h)
    scattered(sbuf.at[2, there_z], gathered.at[0], 4).wait_recv()
    across(gathered.at[0], beyond.at[2], 2).start()
    for n in range(3):
        scatter(sbuf.at[n, here_z], plane.at[n], n)
    across(sbuf.at[0, there_z], over.at[0], 0).wait_recv()
    scatter(over.at[0], beyond.at[0], 6)
    scatter(sbuf.at[3, here_z], plane.at[3], 3)
    scattered(sbuf.at[3, there_z], gathered.at[1], 5).wait_recv()
    across(sbuf.at[1, there_z], over.at[1], 1).wait_recv()
    across(gathered.at[1], beyond.at[3], 3).start()
    scatter(over.at[1], beyond.at[1], 7)

    half = columns * ROW * 16

    def unpack(n, slot, tiles):
        fbuf[n, slot] = tiles.astype(jnp.float32).reshape(half, 128)

    for copy in consts:
        copy.wait()
    receive(edges)
    lane = lax.broadcasted_iota(jnp.int32, (16, 128), 1)
    wide = jnp.where(lane < 8 * REACH, near[1], jnp.where(lane >= 128 - 8 * REACH, near[0], 4096.0))
    near[0] = wide
    rows = lax.broadcasted_iota(jnp.int32, (SPLIT, 1), 0).astype(jnp.float32)

    for k in range(2):
        scattered(sbuf.at[k, here_z], plane.at[k], k).wait_recv()
        unpack(k, 0, plane[k])
        scattered(over.at[k], beyond.at[k], 6 + k).wait_recv()
        unpack(k, 1, beyond[k])

    def window(b, g):
        sm = jnp.dot(ebuf[b], smooth[:, g * 128 : (g + 1) * 128], preferred_element_type=jnp.float32)
        source = win if g == 0 else near.at[0]
        low, high = source[pl.ds(b, 1), :], source[pl.ds(b + 8, 1), :]
        v = jnp.where((rows >= low) & (rows < high), sm, 0.0)
        e = jnp.sum(v, axis=0, keepdims=True)
        m = jnp.sum(v * rows, axis=0, keepdims=True) + (0.5 - low) * e
        acc[g, pl.ds(b, 1), :] = e
        acc[g, pl.ds(b + 8, 1), :] = m

    def gather(half_of, pair, slot, late):
        base = (slot * 2 + late) * 2 * 2 * size
        for i in range(2):
            for j in range(2):
                for h in range(2):
                    q = pair * 2 + h
                    n, at_row = (2 + half_of, j * 4 + q) if late else (j, half_of * 4 + q)
                    part = fbuf[n, slot, pl.ds(i * 8 + at_row, size, stride=16), :]
                    rhs[pair, pl.ds(base + (i * 2 + j) * size, size), h * 128 : (h + 1) * 128] = part.astype(jnp.bfloat16)

    def prepare(half_of, pair):
        for slot, late in ((0, 0), (0, 1), (1, 0)):
            gather(half_of, pair, slot, late)
        span = 8 * size
        sums[pair] = jnp.dot(first[here_z], rhs[pair, :span], preferred_element_type=jnp.float32) + jnp.dot(
            first[there_z, :, : span // 2], rhs[pair, span : span * 3 // 2], preferred_element_type=jnp.float32)

    def transform(half_of, pair):
        gather(half_of, pair, 1, 1)
        span = 8 * size
        out = sums[pair] + jnp.dot(
            first[there_z, :, span // 2 :], rhs[pair, span * 3 // 2 :], preferred_element_type=jnp.float32)
        for h in range(2):
            re, im = out[:SPLIT, h * 128 : (h + 1) * 128], out[SPLIT:, h * 128 : (h + 1) * 128]
            c, s = twiddle[0], twiddle[1]
            z = jnp.concatenate([re * c - im * s, re * s + im * c], axis=1).astype(jnp.bfloat16)
            w = jnp.dot(z, second[...], preferred_element_type=jnp.float32)
            wr, wi = w[:, :128], w[:, 128:]
            ebuf[half_of * 4 + pair * 2 + h] = (wr * wr + wi * wi).astype(jnp.bfloat16)
            window(half_of * 4 + pair * 2 + h, 1)

    partial = beside(acc.at[1], hrecv, hsem, gsem)
    for h in range(2):
        scattered(sbuf.at[2 + h, here_z], plane.at[2 + h], 2 + h).wait_recv()
        unpack(2 + h, 0, plane[2 + h])
        for pair in range(2):
            prepare(h, pair)
        across(gathered.at[h], beyond.at[2 + h], 2 + h).wait_recv()
        unpack(2 + h, 1, beyond[2 + h])
        for pair in range(2):
            transform(h, pair)

        if h == 1:
            send(partial)

        for q in range(4):
            window(h * 4 + q, 0)

    receive(partial)
    total = acc[0] + jnp.where(lane < 8 * REACH, hrecv[0], 0.0) + jnp.where(lane >= 128 - 8 * REACH, hrecv[1], 0.0)
    rowp = lax.broadcasted_iota(jnp.int32, (16, 128), 0)
    group = jnp.where(lane // 8 == rowp, 1.0, 0.0)
    both = lax.dot_general(
        total, group, (((1,), (1,)), ((), ())), precision=lax.Precision.HIGHEST, preferred_element_type=jnp.float32)
    place = block * 16 + lax.broadcasted_iota(jnp.int32, (8, 16), 1)
    weight = jnp.zeros((8, 16), jnp.float32)
    for j, tap in enumerate(TAPS):
        q = place + (j - REACH)
        weight = weight + jnp.where((q >= 0) & (q < blocks * 16), tap, 0.0)
    scale = (1.0 / (16.0 * SPLIT * BINS)) / weight
    e, m = both[:8] * scale, both[8:] * scale
    widths = tbuf[1].astype(jnp.float32)
    result[0] = m / (widths * (e + 1e-06))
    result[1] = e / widths

    sent(edges)
    sent(partial)
    for k in range(2):
        scattered(sbuf.at[k, here_z], plane.at[k], k).wait_send()
        scattered(sbuf.at[2 + k, here_z], plane.at[2 + k], 2 + k).wait_send()
        scattered(sbuf.at[2 + k, there_z], gathered.at[k], 4 + k).wait_send()
        scattered(over.at[k], beyond.at[k], 6 + k).wait_send()
        across(sbuf.at[k, there_z], over.at[k], k).wait_send()
        across(gathered.at[k], beyond.at[2 + k], 2 + k).wait_send()


def local(bands, blocks, staves, weights, replica, start, length):
    each = weights.shape[1]
    first, twiddle, second, smooth = tables(bands, each)
    vmem, hbm = pl.BlockSpec(memory_space=pltpu.VMEM), pl.BlockSpec(memory_space=pltpu.HBM)
    f32, bf16, dma = jnp.float32, jnp.bfloat16, pltpu.SemaphoreType.DMA
    plane = (bands // 2, 16, 128)
    out = pl.pallas_call(
        functools.partial(kernel, bands, blocks),
        out_shape=jax.ShapeDtypeStruct((2, 8, 16), f32),
        in_specs=[hbm] * 9,
        out_specs=vmem,
        scratch_shapes=[
            pltpu.VMEM(replica.shape, f32),
            pltpu.VMEM((2, 8, 16), jnp.int32),
            pltpu.VMEM((each, 2, 128), f32),
            pltpu.VMEM((16, 128), f32),
            pltpu.VMEM((each, 2, 16, 8, 512), bf16),
            pltpu.VMEM((each, 2, 512, 512), bf16),
            pltpu.VMEM((each, 2, *plane), bf16),
            pltpu.VMEM((2, *plane), bf16),
            pltpu.VMEM((2, *plane), bf16),
            pltpu.VMEM((each, *plane), bf16),
            pltpu.VMEM((each, *plane), bf16),
            pltpu.VMEM((each, 2, bands * 8, 128), f32),
            pltpu.VMEM((2, 2 * each * bands, 256), bf16),
            pltpu.VMEM((2, 2 * SPLIT, 256), f32),
            pltpu.VMEM((8, SPLIT, 128), bf16),
            pltpu.VMEM(first.shape, bf16),
            pltpu.VMEM(twiddle.shape, f32),
            pltpu.VMEM(second.shape, bf16),
            pltpu.VMEM(smooth.shape, bf16),
            pltpu.VMEM((2, 16, 128), f32),
            pltpu.VMEM((2, 16, 128), f32),
            pltpu.VMEM((2, 16, 128), f32),
            dma((3,)), dma((each,)), dma((each,)), dma((4,)),
            dma((8,)), dma((8,)), dma((each,)), dma((each,)),
            dma((2,)), dma((2,)), dma((2,)), dma((2,)),
            pltpu.SemaphoreType.REGULAR((2, 2)),
        ],
        compiler_params=pltpu.CompilerParams(collective_id=0, has_side_effects=True, vmem_limit_bytes=63 << 20),
    )(staves, weights, replica, start.T, length.T, first, twiddle, second, smooth)
    return out[0].T, out[1].T


def solution(mesh):
    in_specs = (
        P(None, "ping", "band", None, None),
        P(None, "band", None, None),
        P(),
        P("ping", "band"),
        P("ping", "band"),
    )
    out_specs = (P("ping", "band"), P("ping", "band"))
    step = functools.partial(local, mesh.shape["band"], mesh.shape["ping"])
    return jax.shard_map(step, mesh=mesh, in_specs=in_specs, out_specs=out_specs, check_vma=False)
```

```python
import functools
import math

import ml_dtypes
import numpy as np

import jax
import jax.numpy as jnp
from jax import lax
from jax.experimental import pallas as pl
from jax.experimental.pallas import tpu as pltpu
from jax.sharding import PartitionSpec as P

MESH = pl.DeviceIdType.MESH
BINS, SPLIT, REACH = 8, 256, 4
ROW = 8
TAPS = (1.0, 2.0, 3.0, 4.0, 5.0, 4.0, 3.0, 2.0, 1.0)


def tables(sources, bands_each):
    total = SPLIT * BINS
    turn = 2.0 * math.pi / total
    t1 = np.arange(SPLIT)
    place = np.arange(sources // 2)
    first = []
    for z in range(2):
        source = (place // ROW * 2 + z) * ROW + place % ROW
        columns = []
        for pair in range(bands_each // 2):
            band = (source[None, :] * bands_each + pair * 2 + np.arange(2)[:, None]).reshape(-1)
            angle = ((t1[:, None] * band[None, :] * BINS) % total) * turn
            cos, sin = np.cos(angle), np.sin(angle)
            columns.append(np.block([[cos, -sin], [sin, cos]]))
        first.append(np.concatenate(columns, axis=1))
    first = np.stack(first)
    lane = np.arange(128)
    ping, small = lane // BINS, lane % BINS
    angle = ((t1[:, None] * small[None, :]) % total) * turn
    twiddle = np.stack([np.cos(angle), np.sin(angle)])
    same = ping[:, None] == ping[None, :]
    angle = ((small[:, None] * small[None, :]) % BINS) * (2.0 * math.pi / BINS)
    cos, sin = np.cos(angle) * same, np.sin(angle) * same
    second = np.block([[cos, sin], [-sin, cos]])
    above, below = ping + 16, ping - 16
    beside = np.where(ping < REACH, above, np.where(ping >= 16 - REACH, below, 1000))
    target = np.concatenate([ping, beside])
    kind = np.concatenate([small, small])
    smooth = np.maximum(5 - np.abs(ping[:, None] - target[None, :]), 0) * (small[:, None] == kind[None, :])
    half = ml_dtypes.bfloat16
    return first.astype(half), twiddle.astype(np.float32), second.astype(half), smooth.astype(half)


def kernel(
    bands, blocks,
    staves, weights, replica, start, length, first_in, twiddle_in, second_in, smooth_in,
    result,
    qbuf, tbuf, rep, win, xbuf, wbuf, sbuf, over, gathered, plane, beyond, fbuf, rhs, sums, ebuf,
    first, twiddle, second, smooth, near, acc, hrecv,
    qsem, xsem, wsem, csem, psend, precv, zsend, zrecv, nsem, msem, hsem, gsem, met,
):
    me, block = lax.axis_index("band"), lax.axis_index("ping")
    each = wbuf.shape[0]
    columns = bands // (2 * ROW)
    here_z = lax.rem(lax.div(me, ROW), 2)
    there_z = 1 - here_z
    y, r = lax.div(me, 2 * ROW), lax.rem(me, ROW)
    mine = y * ROW + r

    def at(y, z, r):
        return {"band": (y * 2 + z) * ROW + r}

    near[...] = jnp.zeros_like(near)
    hrecv[...] = jnp.zeros_like(hrecv)

    barrier = pltpu.get_barrier_semaphore()
    pl.semaphore_signal(barrier, inc=1, device_id=at(y, there_z, r), device_id_type=MESH)

    def along(step):
        place = lax.rem(mine + step + columns * ROW, columns * ROW)
        return at(lax.div(place, ROW), here_z, lax.rem(place, ROW))

    for step in (1, -1, 2, -2, 3, -3, 4, -4):
        pl.semaphore_signal(barrier, inc=1, device_id=along(step), device_id_type=MESH)

    @pl.when(block > 0)
    def _():
        pl.semaphore_signal(barrier, inc=1, device_id={"ping": block - 1}, device_id_type=MESH)

    @pl.when(block < blocks - 1)
    def _():
        pl.semaphore_signal(barrier, inc=1, device_id={"ping": block + 1}, device_id_type=MESH)

    loads = []
    for k in range(each):
        loads.append([
            pltpu.make_async_copy(staves.at[:, :, k], xbuf.at[k], xsem.at[k]),
            pltpu.make_async_copy(weights.at[:, k], wbuf.at[k], wsem.at[k]),
        ])
        for copy in loads[-1]:
            copy.start()
        if k == 0:
            small = [
                pltpu.make_async_copy(a, b, qsem.at[i])
                for i, (a, b) in enumerate([(replica, qbuf), (start, tbuf.at[0]), (length, tbuf.at[1])])
            ]
            for copy in small:
                copy.start()
    consts = [
        pltpu.make_async_copy(a, b, csem.at[i])
        for i, (a, b) in enumerate([(first_in, first), (twiddle_in, twiddle), (second_in, second), (smooth_in, smooth)])
    ]
    for copy in consts:
        copy.start()

    def across(src, dst, n):
        return pltpu.make_async_remote_copy(
            src, dst, zsend.at[n], zrecv.at[n], device_id=at(y, there_z, r), device_id_type=MESH)

    size = columns * ROW

    def scatter(src, dst, n):
        @pl.loop(1, size)
        def _(i):
            place = lax.rem(mine + i, size)
            pltpu.make_async_remote_copy(
                src.at[place], dst.at[mine], psend.at[n], precv.at[n],
                device_id=at(lax.div(place, ROW), here_z, lax.rem(place, ROW)), device_id_type=MESH,
            ).start()

        dst[mine] = src[mine]

    def scattered(src, dst, n):
        rest = pl.ds(0, size - 1)
        return pltpu.make_async_remote_copy(
            src.at[rest], dst.at[rest], psend.at[n], precv.at[n],
            device_id=at(y, here_z, lax.rem(r + 1, ROW)), device_id_type=MESH)

    sides = (block > 0).astype(jnp.int32) + (block < blocks - 1).astype(jnp.int32)

    def beside(src, dst, up_sems, down_sems):
        up = pltpu.make_async_remote_copy(
            src, dst.at[0], up_sems.at[0], down_sems.at[0], device_id={"ping": block + 1}, device_id_type=MESH)
        down = pltpu.make_async_remote_copy(
            src, dst.at[1], up_sems.at[1], down_sems.at[1], device_id={"ping": block - 1}, device_id_type=MESH)
        return up, down

    def send(copies):
        @pl.when(block < blocks - 1)
        def _():
            copies[0].start()

        @pl.when(block > 0)
        def _():
            copies[1].start()

    def receive(copies):
        @pl.when(block > 0)
        def _():
            copies[0].wait_recv()

        @pl.when(block < blocks - 1)
        def _():
            copies[1].wait_recv()

    def sent(copies):
        @pl.when(block < blocks - 1)
        def _():
            copies[0].wait_send()

        @pl.when(block > 0)
        def _():
            copies[1].wait_send()

    edges = beside(win, near, nsem, msem)

    for copy in small:
        copy.wait()
    span = each * BINS
    spread = functools.partial(jnp.dot, precision=lax.Precision.HIGHEST, preferred_element_type=jnp.float32)
    row, column = (lax.broadcasted_iota(jnp.int32, (128, 128), d) for d in (0, 1))
    per_tile = 128 // span
    part = qbuf[:, pl.ds(pl.multiple_of(lax.div(me, per_tile) * 128, 128), 128)]
    for k in range(each):
        pick = jnp.where(row == lax.rem(me, per_tile) * span + k * BINS + lax.rem(column, BINS), 1.0, 0.0)
        rep[k] = spread(part, pick)
    row, column = (lax.broadcasted_iota(jnp.int32, (16, 128), d) for d in (0, 1))
    pick = jnp.where(row == lax.div(column, BINS), 1.0, 0.0)
    times = spread(tbuf[...].astype(jnp.float32).reshape(16, 16), pick)
    low = times[:8] - (lax.rem(column[:8], BINS) * SPLIT).astype(jnp.float32)
    win[0:8] = low
    win[8:16] = low + times[8:]

    def tell(turn):
        for side in range(2):
            pl.semaphore_signal(
                met.at[turn, side], inc=1, device_id=along((4 << turn) * (1 - 2 * side)), device_id_type=MESH)

    def hear(turn):
        for side in range(2):
            pl.semaphore_wait(met.at[turn, side], 1)

    def rows_of(k):
        return xbuf[k].astype(jnp.float32).reshape(2 * 128, -1).astype(jnp.bfloat16)

    def beams(k, c, x):
        r0, r1 = rep[k, 0:1, :], rep[k, 1:2, :]
        here = pl.ds(c * 256, 256)
        p0 = jnp.dot(x, wbuf[k, 0, :, here], preferred_element_type=jnp.float32)
        p1 = jnp.dot(x, wbuf[k, 1, :, here], preferred_element_type=jnp.float32)
        re = (p0[:128] - p1[128:]).astype(jnp.bfloat16).T.astype(jnp.float32)
        im = (p1[:128] + p0[128:]).astype(jnp.bfloat16).T.astype(jnp.float32)
        return (re * r0 + im * r1).reshape(32, 8, 128), (im * r0 - re * r1).reshape(32, 8, 128)

    def put(n, c, parts):
        tiles = jnp.concatenate(parts, axis=1).astype(jnp.bfloat16)
        for i in range(4):
            sbuf[n, i % 2, (c * 2 + i // 2) * ROW : (c * 2 + i // 2 + 1) * ROW] = tiles[i * ROW : (i + 1) * ROW]

    chunks = wbuf.shape[-1] // 256

    def early(k):
        for copy in loads[k]:
            copy.wait()
        x = rows_of(k)
        for c in range(chunks):
            put(k, c, beams(k, c, x))

    early(0)
    pl.semaphore_wait(barrier, 9 + sides)
    tell(0)
    across(sbuf.at[0, there_z], over.at[0], 0).start()
    send(edges)
    early(1)
    across(sbuf.at[1, there_z], over.at[1], 1).start()
    hear(0)
    tell(1)
    for k in (2, 3):
        for copy in loads[k]:
            copy.wait()
    x2, x3 = rows_of(2), rows_of(3)
    for c in range(chunks):
        a, b = beams(2, c, x2), beams(3, c, x3)
        for h in range(2):
            part = slice(4 * h, 4 * h + 4)
            put(2 + h, c, [a[0][:, part], b[0][:, part], a[1][:, part], b[1][:, part]])
    hear(1)
    for h in range(2):
        scatter(sbuf.at[2 + h, there_z], gathered.at[h], 4 + h)
    scattered(sbuf.at[2, there_z], gathered.at[0], 4).wait_recv()
    across(gathered.at[0], beyond.at[2], 2).start()
    for n in range(3):
        scatter(sbuf.at[n, here_z], plane.at[n], n)
    across(sbuf.at[0, there_z], over.at[0], 0).wait_recv()
    scatter(over.at[0], beyond.at[0], 6)
    scatter(sbuf.at[3, here_z], plane.at[3], 3)
    scattered(sbuf.at[3, there_z], gathered.at[1], 5).wait_recv()
    across(sbuf.at[1, there_z], over.at[1], 1).wait_recv()
    across(gathered.at[1], beyond.at[3], 3).start()
    scatter(over.at[1], beyond.at[1], 7)

    half = columns * ROW * 16

    def unpack(n, slot, tiles):
        fbuf[n, slot] = tiles.astype(jnp.float32).reshape(half, 128)

    for copy in consts:
        copy.wait()
    receive(edges)
    lane = lax.broadcasted_iota(jnp.int32, (16, 128), 1)
    wide = jnp.where(lane < 8 * REACH, near[1], jnp.where(lane >= 128 - 8 * REACH, near[0], 4096.0))
    near[0] = wide
    rows = lax.broadcasted_iota(jnp.int32, (SPLIT, 1), 0).astype(jnp.float32)

    for k in range(2):
        scattered(sbuf.at[k, here_z], plane.at[k], k).wait_recv()
        unpack(k, 0, plane[k])
        scattered(over.at[k], beyond.at[k], 6 + k).wait_recv()
        unpack(k, 1, beyond[k])

    def window(b, g):
        sm = jnp.dot(ebuf[b], smooth[:, g * 128 : (g + 1) * 128], preferred_element_type=jnp.float32)
        source = win if g == 0 else near.at[0]
        low, high = source[pl.ds(b, 1), :], source[pl.ds(b + 8, 1), :]
        v = jnp.where((rows >= low) & (rows < high), sm, 0.0)
        e = jnp.sum(v, axis=0, keepdims=True)
        m = jnp.sum(v * rows, axis=0, keepdims=True) + (0.5 - low) * e
        acc[g, pl.ds(b, 1), :] = e
        acc[g, pl.ds(b + 8, 1), :] = m

    def gather(half_of, pair, slot, late):
        base = (slot * 2 + late) * 2 * 2 * size
        for i in range(2):
            for j in range(2):
                for h in range(2):
                    q = pair * 2 + h
                    n, at_row = (2 + half_of, j * 4 + q) if late else (j, half_of * 4 + q)
                    part = fbuf[n, slot, pl.ds(i * 8 + at_row, size, stride=16), :]
                    rhs[pair, pl.ds(base + (i * 2 + j) * size, size), h * 128 : (h + 1) * 128] = part.astype(jnp.bfloat16)

    def prepare(half_of, pair):
        for slot, late in ((0, 0), (0, 1), (1, 0)):
            gather(half_of, pair, slot, late)
        span = 8 * size
        sums[pair] = jnp.dot(first[here_z], rhs[pair, :span], preferred_element_type=jnp.float32) + jnp.dot(
            first[there_z, :, : span // 2], rhs[pair, span : span * 3 // 2], preferred_element_type=jnp.float32)

    def transform(half_of, pair):
        gather(half_of, pair, 1, 1)
        span = 8 * size
        out = sums[pair] + jnp.dot(
            first[there_z, :, span // 2 :], rhs[pair, span * 3 // 2 :], preferred_element_type=jnp.float32)
        for h in range(2):
            re, im = out[:SPLIT, h * 128 : (h + 1) * 128], out[SPLIT:, h * 128 : (h + 1) * 128]
            c, s = twiddle[0], twiddle[1]
            z = jnp.concatenate([re * c - im * s, re * s + im * c], axis=1).astype(jnp.bfloat16)
            w = jnp.dot(z, second[...], preferred_element_type=jnp.float32)
            wr, wi = w[:, :128], w[:, 128:]
            ebuf[half_of * 4 + pair * 2 + h] = (wr * wr + wi * wi).astype(jnp.bfloat16)
            window(half_of * 4 + pair * 2 + h, 1)

    partial = beside(acc.at[1], hrecv, hsem, gsem)
    for h in range(2):
        scattered(sbuf.at[2 + h, here_z], plane.at[2 + h], 2 + h).wait_recv()
        unpack(2 + h, 0, plane[2 + h])
        for pair in range(2):
            prepare(h, pair)
        across(gathered.at[h], beyond.at[2 + h], 2 + h).wait_recv()
        unpack(2 + h, 1, beyond[2 + h])
        for pair in range(2):
            transform(h, pair)

        if h == 1:
            send(partial)

        for q in range(4):
            window(h * 4 + q, 0)

    receive(partial)
    total = acc[0] + jnp.where(lane < 8 * REACH, hrecv[0], 0.0) + jnp.where(lane >= 128 - 8 * REACH, hrecv[1], 0.0)
    rowp = lax.broadcasted_iota(jnp.int32, (16, 128), 0)
    group = jnp.where(lane // 8 == rowp, 1.0, 0.0)
    both = lax.dot_general(
        total, group, (((1,), (1,)), ((), ())), precision=lax.Precision.HIGHEST, preferred_element_type=jnp.float32)
    place = block * 16 + lax.broadcasted_iota(jnp.int32, (8, 16), 1)
    weight = jnp.zeros((8, 16), jnp.float32)
    for j, tap in enumerate(TAPS):
        q = place + (j - REACH)
        weight = weight + jnp.where((q >= 0) & (q < blocks * 16), tap, 0.0)
    scale = (1.0 / (16.0 * SPLIT * BINS)) / weight
    e, m = both[:8] * scale, both[8:] * scale
    widths = tbuf[1].astype(jnp.float32)
    result[0] = m / (widths * (e + 1e-06))
    result[1] = e / widths

    sent(edges)
    sent(partial)
    for k in range(2):
        scattered(sbuf.at[k, here_z], plane.at[k], k).wait_send()
        scattered(sbuf.at[2 + k, here_z], plane.at[2 + k], 2 + k).wait_send()
        scattered(sbuf.at[2 + k, there_z], gathered.at[k], 4 + k).wait_send()
        scattered(over.at[k], beyond.at[k], 6 + k).wait_send()
        across(sbuf.at[k, there_z], over.at[k], k).wait_send()
        across(gathered.at[k], beyond.at[2 + k], 2 + k).wait_send()


def local(bands, blocks, staves, weights, replica, start, length):
    each = weights.shape[1]
    first, twiddle, second, smooth = tables(bands, each)
    vmem, hbm = pl.BlockSpec(memory_space=pltpu.VMEM), pl.BlockSpec(memory_space=pltpu.HBM)
    f32, bf16, dma = jnp.float32, jnp.bfloat16, pltpu.SemaphoreType.DMA
    plane = (bands // 2, 16, 128)
    out = pl.pallas_call(
        functools.partial(kernel, bands, blocks),
        out_shape=jax.ShapeDtypeStruct((2, 8, 16), f32),
        in_specs=[hbm] * 9,
        out_specs=vmem,
        scratch_shapes=[
            pltpu.VMEM(replica.shape, f32),
            pltpu.VMEM((2, 8, 16), jnp.int32),
            pltpu.VMEM((each, 2, 128), f32),
            pltpu.VMEM((16, 128), f32),
            pltpu.VMEM((each, 2, 16, 8, 512), bf16),
            pltpu.VMEM((each, 2, 512, 512), bf16),
            pltpu.VMEM((each, 2, *plane), bf16),
            pltpu.VMEM((2, *plane), bf16),
            pltpu.VMEM((2, *plane), bf16),
            pltpu.VMEM((each, *plane), bf16),
            pltpu.VMEM((each, *plane), bf16),
            pltpu.VMEM((each, 2, bands * 8, 128), f32),
            pltpu.VMEM((2, 2 * each * bands, 256), bf16),
            pltpu.VMEM((2, 2 * SPLIT, 256), f32),
            pltpu.VMEM((8, SPLIT, 128), bf16),
            pltpu.VMEM(first.shape, bf16),
            pltpu.VMEM(twiddle.shape, f32),
            pltpu.VMEM(second.shape, bf16),
            pltpu.VMEM(smooth.shape, bf16),
            pltpu.VMEM((2, 16, 128), f32),
            pltpu.VMEM((2, 16, 128), f32),
            pltpu.VMEM((2, 16, 128), f32),
            dma((3,)), dma((each,)), dma((each,)), dma((4,)),
            dma((8,)), dma((8,)), dma((each,)), dma((each,)),
            dma((2,)), dma((2,)), dma((2,)), dma((2,)),
            pltpu.SemaphoreType.REGULAR((2, 2)),
        ],
        compiler_params=pltpu.CompilerParams(collective_id=0, has_side_effects=True, vmem_limit_bytes=63 << 20),
    )(staves, weights, replica, start.T, length.T, first, twiddle, second, smooth)
    return out[0].T, out[1].T


def solution(mesh):
    in_specs = (
        P(None, "ping", "band", None, None),
        P(None, "band", None, None),
        P(),
        P("ping", "band"),
        P("ping", "band"),
    )
    out_specs = (P("ping", "band"), P("ping", "band"))
    step = functools.partial(local, mesh.shape["band"], mesh.shape["ping"])
    return jax.shard_map(step, mesh=mesh, in_specs=in_specs, out_specs=out_specs, check_vma=False)
```
